128 devices in a mesh: dp: 8 (over x, core), shard: 16 (over z, y).
Axes of the slice: x: 4, y: 4, z: 4, core: 2. Of those that a mesh axis runs over, the one named last changes fastest.
Arguments:
- partials: bfloat16 [8, 16, 1024, 3968], P('dp', 'shard'), may hold values from -6 to 6
- error: float32 [8, 1024, 3968], P('dp', 'shard'), may hold values from -4 to 4
- basis: float32 [3968, 32], replicated, may hold values from -6 to 6
Outputs:
- approx_grad: bfloat16 [1024, 3968], P('shard')
- error_next: float32 [8, 1024, 3968], P('dp', 'shard')
- basis_next: float32 [3968, 32], replicated
The draws below stay inside these ranges and needn't reach their ends.
All inputs are finite; a program needn't handle non-finite values.
Results may differ from the reference program's by a relative error of at most 0.0012.
Values sent between devices are 32-bit elements; how exact they have to be, the bound alone decides.
No kernel may reach another device: no remote copies, remote signals or barrier semaphores. Data moves between devices by JAX's collectives and lax.ppermute only.
A program may use at most 128 MiB of HBM per device.

```python
import jax
import jax.numpy as jnp
from jax import lax

D = 3968
RANK = 32
ROWS = 1024
REPLICAS = 8
MEMBERS = 16


def block_levels(stream_key, extent, pieces, low, largest):
    def one(dim, blocks):
        heights = jax.random.uniform(jax.random.fold_in(jax.random.fold_in(stream_key, 6), dim), (blocks,), jnp.float32, low / len(pieces), largest / len(pieces))
        return jnp.repeat(jnp.exp(heights), extent[dim] // blocks).reshape((-1,) + (1,) * (len(extent) - dim - 1))

    loudness = one(*pieces[0])
    for cut in pieces[1:]:
        loudness = loudness * one(*cut)
    return loudness


def centred(key, extent, scale, reach, split=(), dtype=jnp.bfloat16):
    array = scale * jax.random.normal(key, extent, jnp.float32)
    if split:
        array = array * block_levels(key, extent, split, -0.22, 0.18)
    return jnp.clip(array, -reach, reach).astype(dtype)


def setup_inputs(seed: int = 0) -> dict:
    key_list = jax.random.split(jax.random.key(seed), 4)
    partials = centred(key_list[0], (REPLICAS, MEMBERS, ROWS, D), 1.0, 6.0, ((0, 8), (1, 16)))
    error = centred(key_list[1], (REPLICAS, ROWS, D), 0.5, 4.0, ((0, 8), (1, 16)), jnp.float32)
    basis = centred(key_list[2], (D, RANK), 1.0, 6.0, (), jnp.float32)
    return dict(partials=partials, error=error, basis=basis)


def orthonormal(pmat):
    count = pmat.shape[1]
    order = jnp.arange(count)

    def sweep(index, mat):
        column = lax.dynamic_slice_in_dim(mat, index, 1, 1)[:, 0]
        products = jnp.dot(column, mat, precision=lax.Precision.HIGHEST)
        own_norm = lax.dynamic_slice_in_dim(products, index, 1, 0)[0]
        weights = jnp.where(order > index, products / own_norm, jnp.zeros_like(products))
        mat = mat - column[:, None] * weights[None, :]
        scaled = column / jnp.sqrt(own_norm)
        return lax.dynamic_update_slice_in_dim(mat, scaled[:, None], index, 1)
    return lax.fori_loop(0, count, sweep, pmat)

def reference(partials, error, basis):
    grads = lax.optimization_barrier(jnp.sum(partials.astype(jnp.float32), axis=1))
    merged = error + grads
    pmat = jnp.einsum('rnd,dk->nk', merged, basis, precision=lax.Precision.HIGHEST)
    phat = orthonormal(pmat)
    qsum = jnp.einsum('rnd,nk->dk', merged, phat, precision=lax.Precision.HIGHEST)
    approx = jnp.dot(phat, qsum.T, precision=lax.Precision.HIGHEST) / REPLICAS
    return (approx.astype(jnp.bfloat16), merged - approx[None], qsum / REPLICAS)
```

```python
import jax
import jax.numpy as jnp
from jax import lax
from jax.experimental import pallas as pl
from jax.experimental.pallas import tpu as pltpu
from jax.sharding import PartitionSpec as P

BOTH = ("dp", "shard")
SIDE = 4


def place(x, c, z, y):
    return ((x % SIDE) * 2 + c % 2) * SIDE * SIDE + (z % SIDE) * SIDE + y % SIDE


def moved(values, dx=0, dc=0, dz=0, dy=0):
    pairs = [
        (place(x, c, z, y), place(x + dx, c + dc, z + dz, y + dy))
        for x in range(SIDE)
        for c in range(2)
        for z in range(SIDE)
        for y in range(SIDE)
    ]
    return lax.ppermute(values, BOTH, pairs)


def split3(values):
    high = lax.reduce_precision(values, 8, 7)
    rest = values - high
    middle = lax.reduce_precision(rest, 8, 7)
    low = rest - middle
    return [piece.astype(jnp.bfloat16) for piece in (high, middle, low)]


def sum_axis(values, axis):
    ahead = moved(values, **{axis: 1})
    behind = moved(values, **{axis: -1})
    across = moved(values, **{axis: 2})
    return (values + across) + (ahead + behind)


def pick(values, index, size, dim):
    return lax.dynamic_slice_in_dim(values, index * size, size, dim)


def core_scatter(values, core):
    half = values.shape[0] // 2
    other = moved(pick(values, 1 - core, half, 0), dc=1)
    return pick(values, core, half, 0) + other


def core_gather(values, core):
    other = moved(values, dc=1)
    first = jnp.where(core == 0, values, other)
    second = jnp.where(core == 0, other, values)
    return jnp.concatenate([first, second], axis=0)


def sum_left(terms, core):
    half = core_scatter(terms, core)
    for axis in ("dx", "dy", "dz"):
        half = sum_axis(half, axis)
    return core_gather(half, core)


def sum_right(terms, core, x):
    half = core_scatter(terms, core)
    size = half.shape[1] // SIDE
    part = lambda k: pick(half, (x + k) % SIDE, size, 1)
    quarter = (part(0) + moved(part(2), dx=2)) + (
        moved(part(1), dx=1) + moved(part(3), dx=-1)
    )
    for axis in ("dy", "dz"):
        quarter = sum_axis(quarter, axis)
    ring = [quarter, moved(quarter, dx=-1), moved(quarter, dx=2), moved(quarter, dx=1)]
    ring = jnp.stack(ring)
    order = (jnp.arange(SIDE) - x) % SIDE
    whole = jnp.concatenate([lax.dynamic_index_in_dim(ring, order[k], 0, False) for k in range(SIDE)], axis=1)
    return core_gather(whole, core)


def orthonormal_kernel(mat_ref, out_ref, pieces_ref):
    count, rows = mat_ref.shape
    mat = mat_ref[...]
    order = lax.broadcasted_iota(jnp.int32, (count, 1), 0)
    for index in range(count):
        column = mat[index : index + 1, :]
        products = jnp.sum(mat * column, axis=1, keepdims=True)
        own_norm = products[index : index + 1, :]
        weights = jnp.where(order > index, products / own_norm, 0.0)
        scaled = column / jnp.sqrt(own_norm)
        mat = jnp.where(order == index, scaled, mat - weights * column)
    out_ref[...] = mat
    high = mat.astype(jnp.bfloat16)
    rest = mat - high.astype(jnp.float32)
    middle = rest.astype(jnp.bfloat16)
    low = (rest - middle.astype(jnp.float32)).astype(jnp.bfloat16)
    pieces_ref[0:count, :] = high
    pieces_ref[count : 2 * count, :] = middle
    pieces_ref[2 * count : 3 * count, :] = low


def orthonormal(mat):
    count, rows = mat.shape
    return pl.pallas_call(
        orthonormal_kernel,
        out_shape=(
            jax.ShapeDtypeStruct((count, rows), jnp.float32),
            jax.ShapeDtypeStruct((3 * count, rows), jnp.bfloat16),
        ),
        name="orthonormal",
    )(mat)


def shards(partials, error, basis):
    replicas = lax.axis_size("dp")
    dp, shard = lax.axis_index("dp"), lax.axis_index("shard")
    x, core = dp // 2, dp % 2
    partial = partials[0, 0]
    rows, width = partial.shape
    rank = basis.shape[1]
    own = error.shape[1]

    owned_sum = lax.psum_scatter(
        partial.astype(jnp.float32), "shard", scatter_dimension=0, tiled=True
    )

    pieces = jnp.concatenate(split3(basis), axis=1)
    three = jnp.dot(partial, pieces, preferred_element_type=jnp.float32)
    terms = three[:, :rank] + (three[:, rank : 2 * rank] + three[:, 2 * rank :])
    kept = jnp.dot(error[0], basis, precision=lax.Precision.HIGHEST)
    terms = lax.dynamic_update_slice_in_dim(
        terms, pick(terms, shard, own, 0) + kept, shard * own, 0
    )
    pmat = sum_left(terms.T, core)

    phat, phat_pieces = orthonormal(pmat)

    three = jnp.dot(phat_pieces, partial, preferred_element_type=jnp.float32)
    own_phat = pick(phat, shard, own, 1)
    kept = jnp.dot(own_phat, error[0], precision=lax.Precision.HIGHEST)
    terms = kept + (three[:rank] + (three[rank : 2 * rank] + three[2 * rank :]))
    padded = -(-width // (128 * SIDE)) * 128 * SIDE
    terms = jnp.pad(terms, ((0, 0), (0, padded - width)))
    qsum = sum_right(terms, core, x)[:, :width]

    approx = lax.dot_general(
        own_phat, qsum, (((0,), (0,)), ((), ())), precision=lax.Precision.HIGHEST
    ) / replicas
    merged = error[0] + owned_sum
    return (approx.astype(jnp.bfloat16), (merged - approx)[None], qsum.T / replicas)


def solution(mesh):
    return jax.shard_map(
        shards,
        mesh=mesh,
        in_specs=(P("dp", "shard", None, None), P("dp", "shard", None), P()),
        out_specs=(P("shard", None), P("dp", "shard", None), P()),
        check_vma=False,
    )
```

```python
import functools

import jax
import jax.numpy as jnp
from jax import lax
from jax.experimental import pallas as pl
from jax.experimental.pallas import tpu as pltpu
from jax.sharding import PartitionSpec as P

BOTH = ("dp", "shard")
SIDE = 4
LANES = 128
HIGHEST = lax.Precision.HIGHEST
FREE = pl.CostEstimate(flops=0, bytes_accessed=0, transcendentals=0)
ANY = pl.BlockSpec(memory_space=pl.ANY)
WHOLE = pl.BlockSpec(memory_space=pltpu.VMEM)
SCALARS = pl.BlockSpec(memory_space=pltpu.SMEM)


def limit(mebibytes):
    return pltpu.CompilerParams(vmem_limit_bytes=mebibytes << 20)


def place(x, c, z, y):
    return ((x % SIDE) * 2 + c % 2) * SIDE * SIDE + (z % SIDE) * SIDE + y % SIDE


def moved(values, route):
    spots = [
        (x, c, z, y)
        for x in range(SIDE)
        for c in range(2)
        for z in range(SIDE)
        for y in range(SIDE)
    ]
    return lax.ppermute(values, BOTH, [(place(*spot), place(*route(*spot))) for spot in spots])


def other_core(values):
    return moved(values, lambda x, c, z, y: (x, 1 - c, z, y))


def along_x(values, step):
    return moved(values, lambda x, c, z, y: (x + step, c, z, y))


def along_first(values, step):
    return moved(values, lambda x, c, z, y: (x, c, z + step * (1 - c), y + step * c))


def along_second(values, step):
    return moved(values, lambda x, c, z, y: (x, c, z + step * c, y + step * (1 - c)))


def pair_second(values, mask):
    return moved(values, lambda x, c, z, y: (x, c, z ^ (mask * c), y ^ (mask * (1 - c))))


def shape(*dims, dtype=jnp.float32):
    return jax.ShapeDtypeStruct(dims, dtype)


def run(kernel, outs, scalars, operands, after, name, room=8):
    def body(scalar_ref, *refs):
        kernel(scalar_ref, *refs[: len(operands)], *refs[len(operands) + 1 :])

    return pl.pallas_call(
        body,
        in_specs=[SCALARS] + [WHOLE] * len(operands) + [ANY],
        out_specs=[WHOLE] * len(outs),
        out_shape=outs,
        cost_estimate=FREE,
        compiler_params=limit(room),
        name=name,
    )(scalars, *operands, after)


def span(index, size):
    return pl.ds(pl.multiple_of(index * size, size), size)


def combine_kernel(arity, coords_ref, *refs):
    inputs, outputs = refs[: sum(arity)], refs[sum(arity) + 1 :]
    start = 0
    for count, out_ref in zip(arity, outputs):
        own, *came = inputs[start : start + count]
        total = own[0, 0, 0].astype(jnp.float32)
        for ref in came:
            total = total + ref[0]
        out_ref[0] = total
        start += count


def combine(blocks, coords, wanted, after):
    depth, width = blocks.shape[3:]
    cuts = blocks.shape[2] // 2
    arity, operands, specs = [], [], []
    whole = pl.BlockSpec((1, depth, width), lambda k, i, s: (k, i, 0))
    for owner, half, came in wanted:

        def where(k, i, s, owner=owner, half=half):
            core = s[2 * SIDE]
            there = s[owner] * (1 - core) + k * core, s[owner] * core + k * (1 - core)
            return *there, half * cuts + i, 0, 0

        operands += [blocks, *came]
        specs += [pl.BlockSpec((1, 1, 1, depth, width), where)] + [whole] * len(came)
        arity.append(1 + len(came))
    return pl.pallas_call(
        functools.partial(combine_kernel, arity),
        grid_spec=pltpu.PrefetchScalarGridSpec(
            num_scalar_prefetch=1,
            grid=(SIDE, cuts),
            in_specs=specs + [ANY],
            out_specs=[whole] * len(wanted),
        ),
        out_shape=[shape(SIDE, cuts * depth, width)] * len(wanted),
        cost_estimate=FREE,
        compiler_params=limit(8),
        name="combine",
    )(coords, *operands, after)


def turn_kernel(coords_ref, *refs):
    step = pl.program_id(0)
    inputs, outputs = refs[:4], refs[5:]
    for half in (0, 1):
        total = inputs[2 * half][0] + inputs[2 * half + 1][0]
        for spot in range(SIDE):

            @pl.when(step == spot)
            def _(total=total, out_ref=outputs[half * SIDE + spot]):
                out_ref[...] = total


def turn(coords, pairs, after):
    depth, width = pairs[0][0].shape[1:]
    spec = pl.BlockSpec((1, depth, width), lambda k, s: (s[SIDE + k], 0, 0))
    outs = pl.pallas_call(
        turn_kernel,
        grid_spec=pltpu.PrefetchScalarGridSpec(
            num_scalar_prefetch=1,
            grid=(SIDE,),
            in_specs=[spec] * 4 + [ANY],
            out_specs=[pl.BlockSpec((depth, width), lambda k, s: (0, 0))] * (2 * SIDE),
        ),
        out_shape=[shape(depth, width)] * (2 * SIDE),
        cost_estimate=FREE,
        compiler_params=limit(16),
        name="turn",
    )(coords, *pairs[0], *pairs[1], after)
    return outs[:SIDE], outs[SIDE:]


def ring_add_kernel(scalar_ref, *refs):
    up_ref, down_ref = refs[6:]
    depth = refs[0].shape[0]
    up_ref[:depth, :] = refs[0][...] + refs[1][...]
    up_ref[depth:, :] = refs[2][...]
    down_ref[:depth, :] = refs[3][...]
    down_ref[depth:, :] = refs[4][...] + refs[5][...]


def pieces_of(values):
    high = values.astype(jnp.bfloat16)
    rest = values - high.astype(jnp.float32)
    middle = rest.astype(jnp.bfloat16)
    low = (rest - middle.astype(jnp.float32)).astype(jnp.bfloat16)
    return high, middle, low


def left_kernel(scalar_ref, partial_ref, basis_ref, error_ref, after_ref, keep_ref, send_ref, pieces, total):
    step = pl.program_id(0)
    count, own = basis_ref.shape[0], error_ref.shape[0]
    size = partial_ref.shape[0]
    half = count // 2
    across = (((1,), (1,)), ((), ()))

    @pl.when(step == 0)
    def _():
        for index, piece in enumerate(pieces_of(basis_ref[...])):
            pieces[index * count : (index + 1) * count, :] = piece

    three = lax.dot_general(pieces[...], partial_ref[...], across, preferred_element_type=jnp.float32)
    total[:, span(step, size)] = three[:count] + (three[count : 2 * count] + three[2 * count :])

    @pl.when(step == pl.num_programs(0) - 1)
    def _():
        shard, core = scalar_ref[0], scalar_ref[1]
        kept = lax.dot_general(
            basis_ref[...], error_ref[...], across, precision=HIGHEST, preferred_element_type=jnp.float32
        )
        wide = jnp.concatenate([kept] * (LANES // own), axis=1)
        lane = lax.broadcasted_iota(jnp.int32, wide.shape, 1)
        there = span(shard // (LANES // own), LANES)
        total[:, there] += jnp.where(lane // own == shard % (LANES // own), wide, 0.0)
        keep_ref[...] = total[span(core, half), :]
        send_ref[...] = total[span(1 - core, half), :]


def left_terms(scalars, partial, basis, error, after):
    rows, width = partial.shape
    count = basis.shape[0]
    size = rows // SIDE
    fixed = lambda k: (0, 0)
    return pl.pallas_call(
        left_kernel,
        grid=(SIDE,),
        in_specs=[
            SCALARS,
            pl.BlockSpec((size, width), lambda k: (k, 0)),
            pl.BlockSpec(basis.shape, fixed),
            pl.BlockSpec(error.shape, fixed),
            ANY,
        ],
        out_specs=[pl.BlockSpec((count // 2, rows), fixed)] * 2,
        out_shape=[shape(count // 2, rows)] * 2,
        scratch_shapes=[pltpu.VMEM((3 * count, width), jnp.bfloat16), pltpu.VMEM((count, rows), jnp.float32)],
        cost_estimate=FREE,
        compiler_params=limit(24),
        name="left_terms",
    )(scalars, partial, basis, error, after)


def ordered(core, mine, other):
    return jnp.where(core == 0, mine, other), jnp.where(core == 0, other, mine)


def orthonormal_kernel(scalar_ref, mine_ref, other_ref, out_ref, pieces_ref):
    mat = jnp.concatenate(ordered(1 - scalar_ref[1], mine_ref[...], other_ref[...]), axis=0)
    count = mat.shape[0]
    order = lax.broadcasted_iota(jnp.int32, (count, 1), 0)
    for index in range(count):
        column = mat[index : index + 1, :]
        products = jnp.sum(mat * column, axis=1, keepdims=True)
        own_norm = products[index : index + 1, :]
        weights = jnp.where(order > index, products / own_norm, 0.0)
        scaled = column / jnp.sqrt(own_norm)
        mat = jnp.where(order == index, scaled, mat - weights * column)
    out_ref[...] = mat
    for index, piece in enumerate(pieces_of(mat)):
        pieces_ref[index * count : (index + 1) * count, :] = piece


def own_rows(phat, shard, own):
    parts = [phat[:, start : start + own] for start in range(0, LANES, own)]
    chosen = parts[0]
    for index, part in enumerate(parts[1:], 1):
        chosen = jnp.where(shard % (LANES // own) == index, part, chosen)
    return chosen


def right_kernel(scalar_ref, pieces_ref, partial_ref, phat_ref, error_ref, after_ref, keep_ref, send_ref, total):
    step = pl.program_id(0)
    count, own = phat_ref.shape[0], error_ref.shape[0]
    width = partial_ref.shape[1]
    half = count // 2
    three = jnp.dot(pieces_ref[...], partial_ref[...], preferred_element_type=jnp.float32)
    terms = three[:count] + (three[count : 2 * count] + three[2 * count :])

    @pl.when(step == 0)
    def _():
        shard = scalar_ref[0]
        mine = own_rows(phat_ref[:, span(shard // (LANES // own), LANES)], shard, own)
        total[:, :width] = terms + jnp.dot(
            mine, error_ref[...], precision=HIGHEST, preferred_element_type=jnp.float32
        )
        total[:, width:] = jnp.zeros((count, total.shape[1] - width), jnp.float32)

    @pl.when(step > 0)
    def _():
        total[:, :width] += terms

    @pl.when(step == pl.num_programs(0) - 1)
    def _():
        core = scalar_ref[1]
        keep_ref[...] = total[span(core, half), :]
        send_ref[...] = total[span(1 - core, half), :]


def right_terms(scalars, pieces, partial, phat, error, after):
    rows, width = partial.shape
    count = phat.shape[0]
    padded = -(-width // (LANES * SIDE)) * LANES * SIDE
    size = rows // SIDE
    fixed = lambda k: (0, 0)
    return pl.pallas_call(
        right_kernel,
        grid=(SIDE,),
        in_specs=[
            SCALARS,
            pl.BlockSpec((3 * count, size), lambda k: (0, k)),
            pl.BlockSpec((size, width), lambda k: (k, 0)),
            pl.BlockSpec(phat.shape, fixed),
            pl.BlockSpec(error.shape, fixed),
            ANY,
        ],
        out_specs=[pl.BlockSpec((count // 2, padded), fixed)] * 2,
        out_shape=[shape(count // 2, padded)] * 2,
        scratch_shapes=[pltpu.VMEM((count, padded), jnp.float32)],
        cost_estimate=FREE,
        compiler_params=limit(24),
        name="right_terms",
    )(scalars, pieces, partial, phat, error, after)


def add_kernel(scalar_ref, a_ref, b_ref, out_ref):
    out_ref[...] = a_ref[...] + b_ref[...]


def add(scalars, a, b, after):
    return run(add_kernel, [shape(*a.shape)], scalars, [a, b], after, "add")[0]


def add_four_kernel(scalar_ref, a_ref, b_ref, c_ref, d_ref, out_ref):
    out_ref[...] = (a_ref[...] + b_ref[...]) + (c_ref[...] + d_ref[...])


def sum_four(scalars, values, along, after):
    came = [along(values, step) for step in (2, 1, -1)]
    return run(add_four_kernel, [shape(*values.shape)], scalars, [values, *came], after, "add_four")[0]


def add_cut_kernel(scalar_ref, a_ref, b_ref, *out_refs):
    x, size = scalar_ref[2], out_refs[0].shape[1]
    for index, out_ref in enumerate(out_refs):
        there = span(lax.rem(x + index, SIDE), size)
        out_ref[...] = a_ref[:, there] + b_ref[:, there]


def scatter_x(scalars, keep, came, after):
    outs = [shape(keep.shape[0], keep.shape[1] // SIDE)] * SIDE
    parts = run(add_cut_kernel, outs, scalars, [keep, came], after, "add_cut")
    came = [along_x(parts[2], 2), along_x(parts[1], 1), along_x(parts[3], -1)]
    return run(add_four_kernel, outs[:1], scalars, [parts[0], *came], parts[0], "add_four")[0]


def join_kernel(scalar_ref, *refs):
    x, size = scalar_ref[2], refs[0].shape[1]
    for index, ref in enumerate(refs[:-1]):
        refs[-1][:, span(lax.rem(x + index, SIDE), size)] = ref[...]


def gather_x(scalars, values, after):
    came = [along_x(values, -1), along_x(values, 2), along_x(values, 1)]
    outs = [shape(values.shape[0], SIDE * values.shape[1])]
    return run(join_kernel, outs, scalars, [values, *came], after, "join")[0]


def finish_kernel(replicas, scalar_ref, mine_ref, other_ref, phat_ref, error_ref, grad_ref, rest_ref, basis_ref):
    shard, core = scalar_ref[0], scalar_ref[1]
    own, width = error_ref.shape
    right = jnp.concatenate(ordered(core, mine_ref[:, :width], other_ref[:, :width]), axis=0)
    mine = own_rows(phat_ref[:, span(shard // (LANES // own), LANES)], shard, own)
    approx = lax.dot_general(
        mine, right, (((0,), (0,)), ((), ())), precision=HIGHEST, preferred_element_type=jnp.float32
    ) * (1.0 / replicas)
    grad_ref[...] = approx.astype(jnp.bfloat16)
    rest_ref[...] = error_ref[...] - approx
    basis_ref[...] = right * (1.0 / replicas)


def last_kernel(scalar_ref, rest_ref, high_ref, low_ref, up_ref, down_ref, out_ref):
    depth = high_ref.shape[0]
    for index, ref in enumerate((high_ref, low_ref)):
        rows = slice(index * depth, (index + 1) * depth)
        out_ref[rows, :] = rest_ref[rows, :] + (ref[...] + (up_ref[rows, :] + down_ref[rows, :]))


def shards(partials, error, basis):
    replicas = lax.axis_size("dp")
    dp, shard = lax.axis_index("dp"), lax.axis_index("shard")
    x, core = dp // 2, dp % 2
    partial, error, basis = partials[0, 0], error[0], basis.T
    rows, width = partial.shape
    own, count = error.shape[0], basis.shape[0]
    depth = own // 2
    scalars = jnp.stack([shard, core, x]).astype(jnp.int32)
    z, y = shard // SIDE, shard % SIDE
    first, second = jnp.where(core == 0, z, y), jnp.where(core == 0, y, z)
    near = jnp.arange(SIDE)
    coords = jnp.concatenate([(first + near) % SIDE, (second + near) % SIDE, core[None]])
    coords = coords.astype(jnp.int32)
    blocks = partial.reshape(SIDE, SIDE, 4, own // 4, width)

    sent1 = combine(blocks, coords, [(2, 0, []), (2, 1, [])], scalars)
    came1 = [along_first(sent1[0], 1), along_first(sent1[1], -1)]
    keep, send = left_terms(scalars, partial, basis, error, sent1[0])
    part = add(scalars, keep, other_core(send), send)
    part = sum_four(scalars, part, along_x, part)
    part = sum_four(scalars, part, along_second, part)
    sent2 = combine(blocks, coords, [(1, 1, []), (3, 0, [])], part)
    came2 = [along_first(sent2[0], 1), along_first(sent2[1], -1)]
    sent3 = combine(blocks, coords, [(1, 0, [came1[0]]), (3, 1, [came1[1]])], sent2[0])
    came3 = [along_first(sent3[0], 1), along_first(sent3[1], -1)]
    part = other_core(part)
    part = add(scalars, part, pair_second(part, 1), sent3[0])
    part = add(scalars, part, pair_second(part, 3), part)
    phat, pieces = run(
        orthonormal_kernel,
        [shape(count, rows), shape(3 * count, rows, dtype=jnp.bfloat16)],
        scalars,
        [part, other_core(part)],
        part,
        "orthonormal",
    )
    keep, send = right_terms(scalars, pieces, partial, phat, error, phat)
    held = combine(blocks, coords, [(0, 0, [came2[1]]), (0, 1, [came2[0]])], send)
    part = scatter_x(scalars, keep, other_core(send), held[0])
    part = sum_four(scalars, part, along_second, part)
    kept = turn(coords, [(held[0], came3[0]), (held[1], came3[1])], part)
    came4 = [along_second(kept[0][2], 1), along_second(kept[1][2], -1)]
    part = sum_four(scalars, part, along_first, kept[0][0])
    sent5 = run(
        ring_add_kernel,
        [shape(own, width)] * 2,
        scalars,
        [kept[0][1], came4[0], kept[1][1], kept[0][3], kept[1][3], came4[1]],
        part,
        "ring_add",
    )
    came5 = [along_second(sent5[0], 1), along_second(sent5[1], -1)]
    part = gather_x(scalars, part, sent5[0])
    grad, rest, right = run(
        functools.partial(finish_kernel, replicas),
        [shape(own, width, dtype=jnp.bfloat16), shape(own, width), shape(count, width)],
        scalars,
        [part, other_core(part), phat, error],
        part,
        "finish",
        room=24,
    )
    following = run(
        last_kernel,
        [shape(own, width)],
        scalars,
        [rest, kept[0][0], kept[1][0], *came5],
        rest,
        "last",
    )[0]
    return grad, following[None], right.T


def solution(mesh):
    return jax.shard_map(
        shards,
        mesh=mesh,
        in_specs=(P("dp", "shard", None, None), P("dp", "shard", None), P()),
        out_specs=(P("shard", None), P("dp", "shard", None), P()),
        check_vma=False,
    )
```

```python
import functools

import jax
import jax.numpy as jnp
from jax import lax
from jax.experimental import pallas as pl
from jax.experimental.pallas import tpu as pltpu
from jax.sharding import PartitionSpec as P

BOTH = ("dp", "shard")
SIDE = 4
LANES = 128
HIGHEST = lax.Precision.HIGHEST
FREE = pl.CostEstimate(flops=0, bytes_accessed=0, transcendentals=0)
ANY = pl.BlockSpec(memory_space=pl.ANY)
ONCE = pl.Buffered(1)
WHOLE = pl.BlockSpec(memory_space=pltpu.VMEM)
SCALARS = pl.BlockSpec(memory_space=pltpu.SMEM)


def limit(mebibytes):
    return pltpu.CompilerParams(vmem_limit_bytes=mebibytes << 20)


def place(x, c, z, y):
    return ((x % SIDE) * 2 + c % 2) * SIDE * SIDE + (z % SIDE) * SIDE + y % SIDE


def moved(values, route):
    spots = [
        (x, c, z, y)
        for x in range(SIDE)
        for c in range(2)
        for z in range(SIDE)
        for y in range(SIDE)
    ]
    return lax.ppermute(values, BOTH, [(place(*spot), place(*route(*spot))) for spot in spots])


def other_core(values):
    return moved(values, lambda x, c, z, y: (x, 1 - c, z, y))


def along_x(values, step):
    return moved(values, lambda x, c, z, y: (x + step, c, z, y))


def along_first(values, step):
    return moved(values, lambda x, c, z, y: (x, c, z + step * (1 - c), y + step * c))


def along_second(values, step):
    return moved(values, lambda x, c, z, y: (x, c, z + step * c, y + step * (1 - c)))


def pair_second(values, mask):
    return moved(values, lambda x, c, z, y: (x, c, z ^ (mask * c), y ^ (mask * (1 - c))))


def shape(*dims, dtype=jnp.float32):
    return jax.ShapeDtypeStruct(dims, dtype)


def run(kernel, outs, scalars, operands, after, name, room=8, scratch=()):
    after = after if isinstance(after, list) else [after]

    scalars = [] if scalars is None else [scalars]
    count = len(scalars) + len(operands)

    def body(*refs):
        kernel(*refs[:count], *refs[count + len(after) :])

    return pl.pallas_call(
        body,
        in_specs=[SCALARS] * len(scalars) + [WHOLE] * len(operands) + [ANY] * len(after),
        out_specs=[WHOLE] * len(outs),
        out_shape=outs,
        scratch_shapes=list(scratch),
        cost_estimate=FREE,
        compiler_params=limit(room),
        name=name,
    )(*scalars, *operands, *after)


def span(index, size):
    return pl.ds(pl.multiple_of(index * size, size), size)


def combine_kernel(arity, coords_ref, *refs):
    inputs, outputs = refs[: sum(arity)], refs[-len(arity) :]
    start = 0
    for count, out_ref in zip(arity, outputs):
        own, *came = [ref[...] for ref in inputs[start : start + count]]
        total = own[0, 0, 0].astype(jnp.float32)
        for block in came:
            total = total + block[0]
        out_ref[0] = total
        start += count


def combine(blocks, coords, wanted, after):
    after = after if isinstance(after, list) else [after]
    depth, width = blocks.shape[3:]
    cuts = blocks.shape[2] // 2
    arity, operands, specs = [], [], []
    whole = pl.BlockSpec((1, depth, width), lambda k, i, s: (k, i, 0))
    for owner, half, came in wanted:

        def where(k, i, s, owner=owner, half=half):
            there, core = s[owner], s[2 * SIDE]
            return there * (1 - core) + k * core, there * core + k * (1 - core), half * cuts + i, 0, 0

        operands += [blocks, *came]
        specs += [pl.BlockSpec((1, 1, 1, depth, width), where)] + [whole] * len(came)
        arity.append(1 + len(came))
    return pl.pallas_call(
        functools.partial(combine_kernel, arity),
        grid_spec=pltpu.PrefetchScalarGridSpec(
            num_scalar_prefetch=1,
            grid=(SIDE, cuts),
            in_specs=specs + [ANY] * len(after),
            out_specs=[whole] * len(wanted),
        ),
        out_shape=[shape(SIDE, cuts * depth, width)] * len(wanted),
        cost_estimate=FREE,
        compiler_params=limit(8),
        name="combine",
    )(coords, *operands, *after)


def turn_kernel(coords_ref, held_up, came_up, held_down, came_down, up, down, *kept):
    depth = held_up.shape[1]
    there = [coords_ref[SIDE + spot] for spot in range(SIDE)]
    high = lambda spot: held_up[there[spot]] + came_up[there[spot]]
    low = lambda spot: held_down[there[spot]] + came_down[there[spot]]
    up[...] = high(2)
    down[...] = low(2)
    kept[0][:depth, :] = high(1)
    kept[0][depth:, :] = low(1)
    kept[1][:depth, :] = high(3)
    kept[1][depth:, :] = low(3)
    kept[2][:depth, :] = high(0)
    kept[2][depth:, :] = low(0)


def turn(coords, pairs, after):
    depth, width = pairs[0][0].shape[1:]
    outs = [shape(depth, width)] * 2 + [shape(2 * depth, width)] * 3
    return run(turn_kernel, outs, coords, [*pairs[0], *pairs[1]], after, "turn")


def ring_add_kernel(mine_up, came_up, mine_down, came_down, up_ref, down_ref):
    depth = came_up.shape[0]
    up_ref[:depth, :] = mine_up[:depth, :] + came_up[...]
    up_ref[depth:, :] = mine_up[depth:, :]
    down_ref[:depth, :] = mine_down[:depth, :]
    down_ref[depth:, :] = mine_down[depth:, :] + came_down[...]


def pieces_of(values):
    high = values.astype(jnp.bfloat16)
    rest = values - high.astype(jnp.float32)
    middle = rest.astype(jnp.bfloat16)
    low = (rest - middle.astype(jnp.float32)).astype(jnp.bfloat16)
    return high, middle, low


def stacked(values, order):
    pieces = pieces_of(values)
    return [pieces[index] for index in order]


LEFT_ORDER, RIGHT_ORDER = (0, 0, 1, 1, 0, 2), (0, 1, 0, 1, 2, 0)


def left_kernel(scalar_ref, partial_ref, basis_ref, error_ref, after_ref, keep_ref, send_ref, pieces, total):
    step = pl.program_id(0)
    count, own = basis_ref.shape[0], error_ref.shape[0]
    size = partial_ref.shape[0]
    half = count // 2
    across = (((1,), (1,)), ((), ()))

    @pl.when(step == 0)
    def _():
        for index, piece in enumerate(pieces_of(basis_ref[...])):
            pieces[index * count : (index + 1) * count, :] = piece

    three = lax.dot_general(pieces[...], partial_ref[...], across, preferred_element_type=jnp.float32)
    total[:, span(step, size)] = three[:count] + (three[count : 2 * count] + three[2 * count :])

    @pl.when(step == pl.num_programs(0) - 1)
    def _():
        shard, core = scalar_ref[0], scalar_ref[1]
        kept = lax.dot_general(
            basis_ref[...], error_ref[...], across, precision=HIGHEST, preferred_element_type=jnp.float32
        )
        wide = jnp.concatenate([kept] * (LANES // own), axis=1)
        lane = lax.broadcasted_iota(jnp.int32, wide.shape, 1)
        there = span(shard // (LANES // own), LANES)
        total[:, there] += jnp.where(lane // own == shard % (LANES // own), wide, 0.0)
        keep_ref[...] = total[span(core, half), :]
        send_ref[...] = total[span(1 - core, half), :]


def left_terms(scalars, partial, basis, error, after):
    rows, width = partial.shape
    count = basis.shape[0]
    size = rows // SIDE
    fixed = lambda k: (0, 0)
    return pl.pallas_call(
        left_kernel,
        grid=(SIDE,),
        in_specs=[
            SCALARS,
            pl.BlockSpec((size, width), lambda k: (k, 0)),
            pl.BlockSpec(basis.shape, fixed, pipeline_mode=ONCE),
            pl.BlockSpec(error.shape, fixed, pipeline_mode=ONCE),
            ANY,
        ],
        out_specs=[pl.BlockSpec((count // 2, rows), fixed)] * 2,
        out_shape=[shape(count // 2, rows)] * 2,
        scratch_shapes=[pltpu.VMEM((3 * count, width), jnp.bfloat16), pltpu.VMEM((count, rows), jnp.float32)],
        cost_estimate=FREE,
        compiler_params=limit(12),
        name="left_terms",
    )(scalars, partial, basis, error, after)


def ordered(core, mine, other):
    return jnp.where(core == 0, mine, other), jnp.where(core == 0, other, mine)


def orthonormal_kernel(scalar_ref, mine_ref, other_ref, out_ref, pieces_ref):
    mat = jnp.concatenate(ordered(1 - scalar_ref[1], mine_ref[...], other_ref[...]), axis=0)
    count = mat.shape[0]
    order = lax.broadcasted_iota(jnp.int32, (count, 1), 0)
    for index in range(count):
        column = mat[index : index + 1, :]
        products = jnp.sum(mat * column, axis=1, keepdims=True)
        own_norm = products[index : index + 1, :]
        weights = jnp.where(order > index, products / own_norm, 0.0)
        scaled = column / jnp.sqrt(own_norm)
        mat = jnp.where(order == index, scaled, mat - weights * column)
    out_ref[...] = mat
    for index, piece in enumerate(pieces_of(mat)):
        pieces_ref[index * count : (index + 1) * count, :] = piece


def own_rows(phat, shard, own):
    parts = [phat[:, start : start + own] for start in range(0, LANES, own)]
    chosen = parts[0]
    for index, part in enumerate(parts[1:], 1):
        chosen = jnp.where(shard % (LANES // own) == index, part, chosen)
    return chosen


def right_kernel(scalar_ref, pieces_ref, partial_ref, phat_ref, error_ref, after_ref, keep_ref, send_ref, total):
    step = pl.program_id(0)
    count, own = phat_ref.shape[0], error_ref.shape[0]
    width = partial_ref.shape[1]
    half = count // 2
    three = jnp.dot(pieces_ref[...], partial_ref[...], preferred_element_type=jnp.float32)
    terms = three[:count] + (three[count : 2 * count] + three[2 * count :])

    @pl.when(step == 0)
    def _():
        shard = scalar_ref[0]
        mine = own_rows(phat_ref[:, span(shard // (LANES // own), LANES)], shard, own)
        total[:, :width] = terms + jnp.dot(
            mine, error_ref[...], precision=HIGHEST, preferred_element_type=jnp.float32
        )
        total[:, width:] = jnp.zeros((count, total.shape[1] - width), jnp.float32)

    @pl.when(step > 0)
    def _():
        total[:, :width] += terms

    @pl.when(step == pl.num_programs(0) - 1)
    def _():
        core = scalar_ref[1]
        keep_ref[...] = total[span(core, half), :]
        send_ref[...] = total[span(1 - core, half), :]


def right_terms(scalars, pieces, partial, phat, error, after):
    rows, width = partial.shape
    count = phat.shape[0]
    padded = -(-width // (LANES * SIDE)) * LANES * SIDE
    size = rows // SIDE
    fixed = lambda k: (0, 0)
    return pl.pallas_call(
        right_kernel,
        grid=(SIDE,),
        in_specs=[
            SCALARS,
            pl.BlockSpec((3 * count, size), lambda k: (0, k)),
            pl.BlockSpec((size, width), lambda k: (k, 0)),
            pl.BlockSpec(phat.shape, fixed, pipeline_mode=ONCE),
            pl.BlockSpec(error.shape, fixed, pipeline_mode=ONCE),
            ANY,
        ],
        out_specs=[pl.BlockSpec((count // 2, padded), fixed)] * 2,
        out_shape=[shape(count // 2, padded)] * 2,
        scratch_shapes=[pltpu.VMEM((count, padded), jnp.float32)],
        cost_estimate=FREE,
        compiler_params=limit(12),
        name="right_terms",
    )(scalars, pieces, partial, phat, error, after)


def gate(arrays, after):
    return pl.pallas_call(
        lambda *refs: None,
        in_specs=[ANY] * (len(arrays) + len(after)),
        out_specs=[ANY] * len(arrays),
        out_shape=[shape(*array.shape) for array in arrays],
        input_output_aliases={index: index for index in range(len(arrays))},
        cost_estimate=FREE,
        compiler_params=limit(1),
        name="gate",
    )(*arrays, *after)


def add_kernel(*refs):
    terms = [ref[...] for ref in refs[:-1]]
    refs[-1][...] = sum(terms[1:], terms[0])


def add(terms, after):
    return run(add_kernel, [shape(*terms[0].shape)], None, terms, after, "add", room=1)[0]


def add_four_kernel(a_ref, b_ref, c_ref, d_ref, out_ref):
    out_ref[...] = (a_ref[...] + b_ref[...]) + (c_ref[...] + d_ref[...])


def sum_four(values, along, after):
    came = [along(values, step) for step in (2, 1, -1)]
    outs = [shape(*values.shape)]
    return run(add_four_kernel, outs, None, [values, *came], after, "add_four", room=1)[0]


def sum_pairs(values, pairs, after):
    for mask in (1, 3):
        values = after = add([values, pairs(values, mask)], after)
    return values


def add_cut_kernel(scalar_ref, a_ref, b_ref, *out_refs):
    x, size = scalar_ref[2], out_refs[0].shape[1]
    for index, out_ref in enumerate(out_refs):
        there = span(lax.rem(x + index, SIDE), size)
        out_ref[...] = a_ref[:, there] + b_ref[:, there]


def scatter_x(scalars, keep, came, after):
    outs = [shape(keep.shape[0], keep.shape[1] // SIDE)] * SIDE
    parts = run(add_cut_kernel, outs, scalars, [keep, came], after, "add_cut")
    came = [along_x(parts[2], 2), along_x(parts[1], 1), along_x(parts[3], -1)]
    return run(add_four_kernel, outs[:1], None, [parts[0], *came], parts[0], "add_four", room=1)[0]


def join_kernel(scalar_ref, *refs):
    x, size = scalar_ref[2], refs[0].shape[1]
    for index, ref in enumerate(refs[:-1]):
        refs[-1][:, span(lax.rem(x + index, SIDE), size)] = ref[...]


def gather_x(scalars, values, after):
    came = [along_x(values, -1), along_x(values, 2), along_x(values, 1)]
    outs = [shape(values.shape[0], SIDE * values.shape[1])]
    return run(join_kernel, outs, scalars, [values, *came], after, "join")[0]


def finish_kernel(replicas, scalar_ref, mine_ref, other_ref, phat_ref, error_ref, *refs):
    kept_ref, up_ref, down_ref, grad_ref, next_ref, basis_ref = refs
    shard, core = scalar_ref[0], scalar_ref[1]
    own, width = error_ref.shape
    right = jnp.concatenate(ordered(core, mine_ref[:, :width], other_ref[:, :width]), axis=0)
    basis_ref[...] = right * (1.0 / replicas)
    mine = own_rows(phat_ref[:, span(shard // (LANES // own), LANES)], shard, own)
    approx = lax.dot_general(
        jnp.concatenate(stacked(mine, LEFT_ORDER), axis=0),
        jnp.concatenate(stacked(right, RIGHT_ORDER), axis=0),
        (((0,), (0,)), ((), ())),
        preferred_element_type=jnp.float32,
    ) * (1.0 / replicas)
    grad_ref[...] = approx.astype(jnp.bfloat16)
    merged = error_ref[...] + (kept_ref[...] + (up_ref[...] + down_ref[...]))
    next_ref[...] = merged - approx


def shards(partials, error, basis):
    replicas = lax.axis_size("dp")
    dp, shard = lax.axis_index("dp"), lax.axis_index("shard")
    x, core = dp // 2, dp % 2
    partial, error, basis = partials[0, 0], error[0], basis.T
    rows, width = partial.shape
    own, count = error.shape[0], basis.shape[0]
    depth = own // 2
    scalars = jnp.stack([shard, core, x]).astype(jnp.int32)
    z, y = shard // SIDE, shard % SIDE
    first, second = jnp.where(core == 0, z, y), jnp.where(core == 0, y, z)
    near = jnp.arange(SIDE)
    coords = jnp.concatenate([(first + near) % SIDE, (second + near) % SIDE, core[None]])
    coords = coords.astype(jnp.int32)
    blocks = partial.reshape(SIDE, SIDE, 4, own // 4, width)

    sent1 = combine(blocks, coords, [(2, 0, []), (2, 1, [])], scalars)
    came1 = [along_first(sent1[0], 1), along_first(sent1[1], -1)]
    keep, send = left_terms(scalars, partial, basis, error, sent1[0])
    part = add([keep, other_core(send)], keep)
    sent2 = combine(blocks, coords, [(1, 1, []), (3, 0, [])], part)
    part = sum_four(part, along_x, sent2[0])
    sent2 = gate(sent2, [part])
    came2 = [along_first(sent2[0], 1), along_first(sent2[1], -1)]
    part = sum_pairs(part, pair_second, sent2[0])
    sent3 = combine(blocks, coords, [(1, 0, [came1[0]]), (3, 1, [came1[1]])], part)
    (part,) = gate([other_core(part)], [sent3[0]])
    part = sum_four(part, along_second, part)
    sent3 = gate(sent3, [part])
    came3 = [along_first(sent3[0], 1), along_first(sent3[1], -1)]
    phat, pieces = run(
        orthonormal_kernel,
        [shape(count, rows), shape(3 * count, rows, dtype=jnp.bfloat16)],
        scalars,
        [part, other_core(part)],
        sent3[0],
        "orthonormal",
    )
    keep, send = right_terms(scalars, pieces, partial, phat, error, phat)
    held = combine(blocks, coords, [(0, 0, [came2[1]]), (0, 1, [came2[0]])], send)
    part = scatter_x(scalars, keep, other_core(send), held[0])
    part = sum_four(part, along_second, part)
    up, down, *kept = turn(coords, [(held[0], came3[0]), (held[1], came3[1])], part)
    came4 = [along_second(up, 1), along_second(down, -1)]
    part = sum_four(part, along_first, part)
    sent5 = run(
        ring_add_kernel,
        [shape(own, width)] * 2,
        None,
        [kept[0], came4[0], kept[1], came4[1]],
        part,
        "ring_add",
    )
    came5 = [along_second(sent5[0], 1), along_second(sent5[1], -1)]
    part = gather_x(scalars, part, sent5[0])
    grad, following, right = run(
        functools.partial(finish_kernel, replicas),
        [shape(own, width, dtype=jnp.bfloat16), shape(own, width), shape(count, width)],
        scalars,
        [part, other_core(part), phat, error, kept[2], *came5],
        part,
        "finish",
    )
    return grad, following[None], right.T


def solution(mesh):
    return jax.shard_map(
        shards,
        mesh=mesh,
        in_specs=(P("dp", "shard", None, None), P("dp", "shard", None), P()),
        out_specs=(P("shard", None), P("dp", "shard", None), P()),
        check_vma=False,
    )
```

```python
import functools

import jax
import jax.numpy as jnp
from jax import lax
from jax.experimental import pallas as pl
from jax.experimental.pallas import tpu as pltpu
from jax.sharding import PartitionSpec as P

BOTH = ("dp", "shard")
SIDE = 4
LANES = 128
HIGHEST = lax.Precision.HIGHEST
FREE = pl.CostEstimate(flops=0, bytes_accessed=0, transcendentals=0)
ANY = pl.BlockSpec(memory_space=pl.ANY)
ONCE = pl.Buffered(1)
WHOLE = pl.BlockSpec(memory_space=pltpu.VMEM)
SCALARS = pl.BlockSpec(memory_space=pltpu.SMEM)


def limit(mebibytes):
    return pltpu.CompilerParams(vmem_limit_bytes=mebibytes << 20)


def place(x, c, z, y):
    return ((x % SIDE) * 2 + c % 2) * SIDE * SIDE + (z % SIDE) * SIDE + y % SIDE


def moved(values, route):
    spots = [
        (x, c, z, y)
        for x in range(SIDE)
        for c in range(2)
        for z in range(SIDE)
        for y in range(SIDE)
    ]
    return lax.ppermute(values, BOTH, [(place(*spot), place(*route(*spot))) for spot in spots])


def other_core(values):
    return moved(values, lambda x, c, z, y: (x, 1 - c, z, y))


def along_x(values, step):
    return moved(values, lambda x, c, z, y: (x + step, c, z, y))


def along_first(values, step):
    return moved(values, lambda x, c, z, y: (x, c, z + step * (1 - c), y + step * c))


def along_second(values, step):
    return moved(values, lambda x, c, z, y: (x, c, z + step * c, y + step * (1 - c)))


def pair_x(values, mask):
    return moved(values, lambda x, c, z, y: (x ^ mask, c, z, y))


def pair_second(values, mask):
    return moved(values, lambda x, c, z, y: (x, c, z ^ (mask * c), y ^ (mask * (1 - c))))


def shape(*dims, dtype=jnp.float32):
    return jax.ShapeDtypeStruct(dims, dtype)


def run(kernel, outs, scalars, operands, after, name, room=8, scratch=()):
    after = after if isinstance(after, list) else [after]

    scalars = [] if scalars is None else [scalars]
    count = len(scalars) + len(operands)

    def body(*refs):
        kernel(*refs[:count], *refs[count + len(after) :])

    return pl.pallas_call(
        body,
        in_specs=[SCALARS] * len(scalars) + [WHOLE] * len(operands) + [ANY] * len(after),
        out_specs=[WHOLE] * len(outs),
        out_shape=outs,
        scratch_shapes=list(scratch),
        cost_estimate=FREE,
        compiler_params=limit(room),
        name=name,
    )(*scalars, *operands, *after)


def in_hbm(values):
    return pltpu.with_memory_space_constraint(values, pltpu.HBM)


def span(index, size):
    return pl.ds(pl.multiple_of(index * size, size), size)


def combine_kernel(arity, coords_ref, *refs):
    inputs, outputs = refs[: sum(arity)], refs[-len(arity) :]
    start = 0
    for count, out_ref in zip(arity, outputs):
        own, *came = [ref[...] for ref in inputs[start : start + count]]
        total = own[0, 0, 0].astype(jnp.float32)
        for block in came:
            total = total + block[0]
        out_ref[0] = total
        start += count


def combine(blocks, coords, wanted, after):
    after = after if isinstance(after, list) else [after]
    depth, width = blocks.shape[3:]
    cuts = blocks.shape[2] // 2
    arity, operands, specs = [], [], []
    whole = pl.BlockSpec((1, depth, width), lambda k, i, s: (k, i, 0))
    for owner, half, came in wanted:

        def where(k, i, s, owner=owner, half=half):
            there, core = s[owner], s[2 * SIDE]
            return there * (1 - core) + k * core, there * core + k * (1 - core), half * cuts + i, 0, 0

        operands += [blocks, *came]
        specs += [pl.BlockSpec((1, 1, 1, depth, width), where)] + [whole] * len(came)
        arity.append(1 + len(came))
    return pl.pallas_call(
        functools.partial(combine_kernel, arity),
        grid_spec=pltpu.PrefetchScalarGridSpec(
            num_scalar_prefetch=1,
            grid=(SIDE, cuts),
            in_specs=specs + [ANY] * len(after),
            out_specs=[whole] * len(wanted),
        ),
        out_shape=[shape(SIDE, cuts * depth, width)] * len(wanted),
        cost_estimate=FREE,
        compiler_params=limit(8),
        name="combine",
    )(coords, *operands, *after)


def turn_first_kernel(coords_ref, held_up, came_up, held_down, came_down, up, down):
    there = coords_ref[SIDE + 2]
    up[...] = held_up[there] + came_up[there]
    down[...] = held_down[there] + came_down[there]


def turn_rest_kernel(coords_ref, held_up, came_up, held_down, came_down, up, down, kept_up, kept_down, own):
    depth = held_up.shape[1]
    there = [coords_ref[SIDE + spot] for spot in range(SIDE)]
    high = lambda spot: held_up[there[spot]] + came_up[there[spot]]
    low = lambda spot: held_down[there[spot]] + came_down[there[spot]]
    up[...] = low(1)
    down[...] = high(3)
    kept_up[...] = high(1)
    kept_down[...] = low(3)
    own[:depth, :] = high(0)
    own[depth:, :] = low(0)


def turn(coords, pairs, after):
    depth, width = pairs[0][0].shape[1:]
    part, terms = shape(depth, width), [*pairs[0], *pairs[1]]
    first = run(turn_first_kernel, [part] * 2, coords, terms, after, "turn_first")
    outs = [part] * 4 + [shape(2 * depth, width)]
    return [*first, *run(turn_rest_kernel, outs, coords, terms, first[0], "turn_rest")]


def ring_add_kernel(mine_up, came_up, mine_down, came_down, up_ref, down_ref):
    up_ref[...] = mine_up[...] + came_up[...]
    down_ref[...] = mine_down[...] + came_down[...]


def pieces_of(values):
    high = values.astype(jnp.bfloat16)
    rest = values - high.astype(jnp.float32)
    middle = rest.astype(jnp.bfloat16)
    low = (rest - middle.astype(jnp.float32)).astype(jnp.bfloat16)
    return high, middle, low


def stacked(values, order):
    pieces = pieces_of(values)
    return [pieces[index] for index in order]


LEFT_ORDER, RIGHT_ORDER = (0, 0, 1, 1, 0, 2), (0, 1, 0, 1, 2, 0)


def left_kernel(
    scalar_ref, partial_ref, basis_ref, error_ref, after_ref, keep_ref, send_ref, copy_ref, pieces, total
):
    step = pl.program_id(0)
    count, own = basis_ref.shape[0], error_ref.shape[0]
    size = partial_ref.shape[0]
    half = count // 2
    across = (((1,), (1,)), ((), ()))

    @pl.when(step == 0)
    def _():
        for index, piece in enumerate(pieces_of(basis_ref[...])):
            pieces[index * count : (index + 1) * count, :] = piece

    copy_ref[...] = partial_ref[...]
    three = lax.dot_general(pieces[...], partial_ref[...], across, preferred_element_type=jnp.float32)
    total[:, span(step, size)] = three[:count] + (three[count : 2 * count] + three[2 * count :])

    @pl.when(step == pl.num_programs(0) - 1)
    def _():
        shard, core = scalar_ref[0], scalar_ref[1]
        kept = lax.dot_general(
            basis_ref[...], error_ref[...], across, precision=HIGHEST, preferred_element_type=jnp.float32
        )
        wide = jnp.concatenate([kept] * (LANES // own), axis=1)
        lane = lax.broadcasted_iota(jnp.int32, wide.shape, 1)
        there = span(shard // (LANES // own), LANES)
        total[:, there] += jnp.where(lane // own == shard % (LANES // own), wide, 0.0)
        keep_ref[...] = total[span(core, half), :]
        send_ref[...] = total[span(1 - core, half), :]


def left_terms(scalars, partial, basis, error, after):
    rows, width = partial.shape
    count = basis.shape[0]
    size = rows // SIDE
    fixed = lambda k: (0, 0)
    return pl.pallas_call(
        left_kernel,
        grid=(SIDE,),
        in_specs=[
            SCALARS,
            pl.BlockSpec((size, width), lambda k: (k, 0)),
            pl.BlockSpec(basis.shape, fixed, pipeline_mode=ONCE),
            pl.BlockSpec(error.shape, fixed, pipeline_mode=ONCE),
            ANY,
        ],
        out_specs=[pl.BlockSpec((count // 2, rows), fixed)] * 2
        + [pl.BlockSpec((size, width), lambda k: (k, 0))],
        out_shape=[shape(count // 2, rows)] * 2 + [shape(rows, width, dtype=partial.dtype)],
        scratch_shapes=[pltpu.VMEM((3 * count, width), jnp.bfloat16), pltpu.VMEM((count, rows), jnp.float32)],
        cost_estimate=FREE,
        compiler_params=limit(16),
        name="left_terms",
    )(scalars, partial, basis, error, after)


def ordered(core, mine, other):
    return jnp.where(core == 0, mine, other), jnp.where(core == 0, other, mine)


def orthonormal_kernel(scalar_ref, mine_ref, other_ref, out_ref, pieces_ref):
    mat = jnp.concatenate(ordered(1 - scalar_ref[1], mine_ref[...], other_ref[...]), axis=0)
    count = mat.shape[0]
    order = lax.broadcasted_iota(jnp.int32, (count, 1), 0)
    for index in range(count):
        column = mat[index : index + 1, :]
        products = jnp.sum(mat * column, axis=1, keepdims=True)
        own_norm = products[index : index + 1, :]
        weights = jnp.where(order > index, products / own_norm, 0.0)
        scaled = column / jnp.sqrt(own_norm)
        mat = jnp.where(order == index, scaled, mat - weights * column)
    out_ref[...] = mat
    for index, piece in enumerate(pieces_of(mat)):
        pieces_ref[index * count : (index + 1) * count, :] = piece


def own_rows(phat, shard, own):
    parts = [phat[:, start : start + own] for start in range(0, LANES, own)]
    chosen = parts[0]
    for index, part in enumerate(parts[1:], 1):
        chosen = jnp.where(shard % (LANES // own) == index, part, chosen)
    return chosen


def right_kernel(scalar_ref, pieces_ref, partial_ref, phat_ref, error_ref, after_ref, keep_ref, send_ref, total):
    step = pl.program_id(0)
    count, own = phat_ref.shape[0], error_ref.shape[0]
    width = partial_ref.shape[1]
    half = count // 2
    three = jnp.dot(pieces_ref[...], partial_ref[...], preferred_element_type=jnp.float32)
    terms = three[:count] + (three[count : 2 * count] + three[2 * count :])

    @pl.when(step == 0)
    def _():
        shard = scalar_ref[0]
        mine = own_rows(phat_ref[:, span(shard // (LANES // own), LANES)], shard, own)
        total[:, :width] = terms + jnp.dot(
            mine, error_ref[...], precision=HIGHEST, preferred_element_type=jnp.float32
        )
        total[:, width:] = jnp.zeros((count, total.shape[1] - width), jnp.float32)

    @pl.when(step > 0)
    def _():
        total[:, :width] += terms

    @pl.when(step == pl.num_programs(0) - 1)
    def _():
        core = scalar_ref[1]
        keep_ref[...] = total[span(core, half), :]
        send_ref[...] = total[span(1 - core, half), :]


def right_terms(scalars, pieces, partial, phat, error, after):
    rows, width = partial.shape
    count = phat.shape[0]
    padded = -(-width // (LANES * SIDE)) * LANES * SIDE
    size = rows // SIDE
    fixed = lambda k: (0, 0)
    return pl.pallas_call(
        right_kernel,
        grid=(SIDE,),
        in_specs=[
            SCALARS,
            pl.BlockSpec((3 * count, size), lambda k: (0, k)),
            pl.BlockSpec((size, width), lambda k: (k, 0)),
            pl.BlockSpec(phat.shape, fixed, pipeline_mode=ONCE),
            pl.BlockSpec(error.shape, fixed, pipeline_mode=ONCE),
            ANY,
        ],
        out_specs=[pl.BlockSpec((count // 2, padded), fixed)] * 2,
        out_shape=[shape(count // 2, padded)] * 2,
        scratch_shapes=[pltpu.VMEM((count, padded), jnp.float32)],
        cost_estimate=FREE,
        compiler_params=limit(12),
        name="right_terms",
    )(scalars, pieces, partial, phat, error, after)


def gate(arrays, after):
    return pl.pallas_call(
        lambda *refs: None,
        in_specs=[ANY] * (len(arrays) + len(after)),
        out_specs=[ANY] * len(arrays),
        out_shape=[shape(*array.shape) for array in arrays],
        input_output_aliases={index: index for index in range(len(arrays))},
        cost_estimate=FREE,
        compiler_params=limit(1),
        name="gate",
    )(*arrays, *after)


def add_kernel(*refs):
    terms = [ref[...] for ref in refs[:-1]]
    refs[-1][...] = sum(terms[1:], terms[0])


def add(terms, after):
    return run(add_kernel, [shape(*terms[0].shape)], None, terms, after, "add", room=1)[0]


def add_four_kernel(a_ref, b_ref, c_ref, d_ref, out_ref):
    out_ref[...] = (a_ref[...] + b_ref[...]) + (c_ref[...] + d_ref[...])


def sum_four(values, along, after):
    return sum_came(values, [along(values, step) for step in (2, 1, -1)], after)


def sum_came(values, came, after):
    outs = [shape(*values.shape)]
    return run(add_four_kernel, outs, None, [values, *came], after, "add_four", room=1)[0]


def sum_pairs(values, pairs, after):
    for mask in (1, 3):
        values = after = add([values, pairs(values, mask)], after)
    return values


def add_cut_kernel(scalar_ref, a_ref, b_ref, *out_refs):
    x, size = scalar_ref[2], out_refs[0].shape[1]
    for index, out_ref in enumerate(out_refs):
        there = span(lax.rem(x + index, SIDE), size)
        out_ref[...] = a_ref[:, there] + b_ref[:, there]


def scatter_x(scalars, keep, came, after):
    outs = [shape(keep.shape[0], keep.shape[1] // SIDE)] * SIDE
    parts = run(add_cut_kernel, outs, scalars, [keep, came], after, "add_cut")
    came = [along_x(parts[2], 2), along_x(parts[1], 1), along_x(parts[3], -1)]
    return run(add_four_kernel, outs[:1], None, [parts[0], *came], parts[0], "add_four", room=1)[0]


def join_two_kernel(a_ref, b_ref, out_ref):
    size = a_ref.shape[1]
    out_ref[:, :size] = a_ref[...]
    out_ref[:, size:] = b_ref[...]


def join_four_kernel(scalar_ref, mine_ref, came_ref, out_ref):
    x, size = scalar_ref[2], mine_ref.shape[1] // 2
    for ref, masks in ((mine_ref, (0, 3)), (came_ref, (1, 2))):
        for index, mask in enumerate(masks):
            out_ref[:, span(x ^ mask, size)] = ref[:, index * size : (index + 1) * size]


def finish_kernel(replicas, scalar_ref, mine_ref, other_ref, phat_ref, error_ref, *refs):
    kept_ref, up_ref, down_ref, grad_ref, rest_ref, basis_ref = refs
    shard, core = scalar_ref[0], scalar_ref[1]
    own, width = error_ref.shape
    right = jnp.concatenate(ordered(core, mine_ref[:, :width], other_ref[:, :width]), axis=0)
    basis_ref[...] = right * (1.0 / replicas)
    mine = own_rows(phat_ref[:, span(shard // (LANES // own), LANES)], shard, own)
    approx = lax.dot_general(
        jnp.concatenate(stacked(mine, LEFT_ORDER), axis=0),
        jnp.concatenate(stacked(right, RIGHT_ORDER), axis=0),
        (((0,), (0,)), ((), ())),
        preferred_element_type=jnp.float32,
    ) * (1.0 / replicas)
    grad_ref[...] = approx.astype(jnp.bfloat16)
    depth = own // 2
    for rows, came_ref in ((slice(0, depth), down_ref), (slice(depth, own), up_ref)):
        rest_ref[rows, :] = (error_ref[rows, :] + (kept_ref[rows, :] + came_ref[...])) - approx[rows, :]


def last_kernel(rest_ref, up_ref, down_ref, out_ref):
    early = pl.program_id(0) == 0
    out_ref[...] = rest_ref[...] + jnp.where(early, up_ref[...], down_ref[...])


def last_sum(rest, up, down):
    rows, width = rest.shape
    depth = rows // SIDE
    whole = pl.BlockSpec((depth, width), lambda h, i: (2 * h + i, 0))
    return pl.pallas_call(
        last_kernel,
        grid=(2, 2),
        in_specs=[
            whole,
            pl.BlockSpec((depth, width), lambda h, i: (jnp.where(h == 0, i, 1), 0)),
            pl.BlockSpec((depth, width), lambda h, i: (jnp.where(h == 0, 0, i), 0)),
        ],
        out_specs=whole,
        out_shape=shape(rows, width),
        cost_estimate=FREE,
        compiler_params=limit(4),
        name="last_sum",
    )(rest, up, down)


def shards(partials, error, basis):
    replicas = lax.axis_size("dp")
    dp, shard = lax.axis_index("dp"), lax.axis_index("shard")
    x, core = dp // 2, dp % 2
    partial, error, basis = partials[0, 0], error[0], basis.T
    rows, width = partial.shape
    own, count = error.shape[0], basis.shape[0]
    depth = own // 2
    scalars = jnp.stack([shard, core, x]).astype(jnp.int32)
    z, y = shard // SIDE, shard % SIDE
    first, second = jnp.where(core == 0, z, y), jnp.where(core == 0, y, z)
    near = jnp.arange(SIDE)
    coords = jnp.concatenate([(first + near) % SIDE, (second + near) % SIDE, core[None]])
    coords = coords.astype(jnp.int32)
    large = in_hbm(partial.reshape(SIDE, SIDE, 2, own // 2, width))

    sent1 = combine(large, coords, [(2, 0, []), (2, 1, [])], scalars)
    came1 = [along_first(sent1[0], 1), along_first(sent1[1], -1)]
    keep, send, partial = left_terms(scalars, in_hbm(partial), basis, error, sent1[0])
    blocks = partial.reshape(SIDE, SIDE, 4, own // 4, width)
    part = add([keep, other_core(send)], keep)
    sent2 = combine(blocks, coords, [(1, 1, []), (3, 0, [])], part)
    part = sum_four(part, along_x, sent2[0])
    sent2 = gate(sent2, [part])
    came2 = [along_first(sent2[0], 1), along_first(sent2[1], -1)]
    part = sum_pairs(part, pair_second, sent2[0])
    sent3 = combine(blocks, coords, [(1, 0, [came1[0]]), (3, 1, [came1[1]])], part)
    (part,) = gate([other_core(part)], [sent3[0]])
    part = sum_four(part, along_second, part)
    sent3 = gate(sent3, [part])
    came3 = [along_first(sent3[0], 1), along_first(sent3[1], -1)]
    phat, pieces = run(
        orthonormal_kernel,
        [shape(count, rows), shape(3 * count, rows, dtype=jnp.bfloat16)],
        scalars,
        [part, other_core(part)],
        sent3[0],
        "orthonormal",
    )
    keep, send = right_terms(scalars, pieces, partial, phat, error, phat)
    held = combine(blocks, coords, [(0, 0, [came2[1]]), (0, 1, [came2[0]])], send)
    part = scatter_x(scalars, keep, other_core(send), held[0])
    part = sum_four(part, along_second, part)
    came = [along_first(part, step) for step in (2, 1, -1)]
    up, down, up_local, down_local, kept_up, kept_down, kept = turn(
        coords, [(held[0], came3[0]), (held[1], came3[1])], came
    )
    came4 = [along_second(up, 1), along_second(down, -1)]
    came5 = [along_second(up_local, 1), along_second(down_local, -1)]
    part = sum_came(part, came, kept)
    pair = run(join_two_kernel, [shape(count // 2, 2 * part.shape[1])], None, [part, pair_x(part, 3)], part, "join", room=1)[0]
    sent6 = run(
        ring_add_kernel,
        [shape(own // 2, width)] * 2,
        None,
        [kept_up, came4[0], kept_down, came4[1]],
        pair,
        "ring_add",
    )
    came6 = [along_second(sent6[0], 1), along_second(sent6[1], -1)]
    outs = [shape(count // 2, 2 * pair.shape[1])]
    part = run(join_four_kernel, outs, scalars, [pair, pair_x(pair, 1)], sent6[0], "join")[0]
    grad, rest, right = run(
        functools.partial(finish_kernel, replicas),
        [shape(own, width, dtype=jnp.bfloat16), shape(own, width), shape(count, width)],
        scalars,
        [part, other_core(part), phat, error, kept, *came5],
        part,
        "finish",
    )
    return grad, last_sum(rest, *came6)[None], right.T


def solution(mesh):
    return jax.shard_map(
        shards,
        mesh=mesh,
        in_specs=(P("dp", "shard", None, None), P("dp", "shard", None), P()),
        out_specs=(P("shard", None), P("dp", "shard", None), P()),
        check_vma=False,
    )
```

```python
import functools

import jax
import jax.numpy as jnp
from jax import lax
from jax.experimental import pallas as pl
from jax.experimental.pallas import tpu as pltpu
from jax.sharding import PartitionSpec as P

BOTH = ("dp", "shard")
SIDE = 4
LANES = 128
SUBLANES = 8
HIGHEST = lax.Precision.HIGHEST
FREE = pl.CostEstimate(flops=0, bytes_accessed=0, transcendentals=0)
ANY = pl.BlockSpec(memory_space=pl.ANY)
ONCE = pl.Buffered(1)
WHOLE = pl.BlockSpec(memory_space=pltpu.VMEM)
SCALARS = pl.BlockSpec(memory_space=pltpu.SMEM)


def limit(mebibytes):
    return pltpu.CompilerParams(vmem_limit_bytes=mebibytes << 20)


def place(x, c, z, y):
    return ((x % SIDE) * 2 + c % 2) * SIDE * SIDE + (z % SIDE) * SIDE + y % SIDE


def moved(values, route):
    spots = [
        (x, c, z, y)
        for x in range(SIDE)
        for c in range(2)
        for z in range(SIDE)
        for y in range(SIDE)
    ]
    return lax.ppermute(values, BOTH, [(place(*spot), place(*route(*spot))) for spot in spots])


def other_core(values):
    return moved(values, lambda x, c, z, y: (x, 1 - c, z, y))


def along_x(values, step):
    return moved(values, lambda x, c, z, y: (x + step, c, z, y))


def along_first(values, step):
    return moved(values, lambda x, c, z, y: (x, c, z + step * (1 - c), y + step * c))


def along_second(values, step):
    return moved(values, lambda x, c, z, y: (x, c, z + step * c, y + step * (1 - c)))


def pair_x(values, mask):
    return moved(values, lambda x, c, z, y: (x ^ mask, c, z, y))


def pair_second(values, mask):
    return moved(values, lambda x, c, z, y: (x, c, z ^ (mask * c), y ^ (mask * (1 - c))))


def shape(*dims, dtype=jnp.float32):
    return jax.ShapeDtypeStruct(dims, dtype)


def run(kernel, outs, scalars, operands, after, name, room=8, scratch=()):
    after = after if isinstance(after, list) else [after]

    scalars = [] if scalars is None else [scalars]
    count = len(scalars) + len(operands)

    def body(*refs):
        kernel(*refs[:count], *refs[count + len(after) :])

    return pl.pallas_call(
        body,
        in_specs=[SCALARS] * len(scalars) + [WHOLE] * len(operands) + [ANY] * len(after),
        out_specs=[WHOLE] * len(outs),
        out_shape=outs,
        scratch_shapes=list(scratch),
        cost_estimate=FREE,
        compiler_params=limit(room),
        name=name,
    )(*scalars, *operands, *after)


def in_hbm(values):
    return pltpu.with_memory_space_constraint(values, pltpu.HBM)


def span(index, size):
    return pl.ds(pl.multiple_of(index * size, size), size)


def combine_kernel(arity, coords_ref, *refs):
    inputs, outputs = refs[: sum(arity)], refs[-len(arity) :]
    start = 0
    for count, out_ref in zip(arity, outputs):
        own, *came = [ref[...] for ref in inputs[start : start + count]]
        total = own[0, 0, 0].astype(jnp.float32)
        for block in came:
            total = total + block[0]
        out_ref[0] = total
        start += count


def combine(blocks, coords, wanted, after):
    after = after if isinstance(after, list) else [after]
    depth, width = blocks.shape[3:]
    cuts = blocks.shape[2] // 2
    arity, operands, specs = [], [], []
    whole = pl.BlockSpec((1, depth, width), lambda k, i, s: (k, i, 0))
    for owner, half, came in wanted:

        def where(k, i, s, owner=owner, half=half):
            there, core = s[owner], s[2 * SIDE]
            return there * (1 - core) + k * core, there * core + k * (1 - core), half * cuts + i, 0, 0

        operands += [blocks, *came]
        specs += [pl.BlockSpec((1, 1, 1, depth, width), where)] + [whole] * len(came)
        arity.append(1 + len(came))
    return pl.pallas_call(
        functools.partial(combine_kernel, arity),
        grid_spec=pltpu.PrefetchScalarGridSpec(
            num_scalar_prefetch=1,
            grid=(SIDE, cuts),
            in_specs=specs + [ANY] * len(after),
            out_specs=[whole] * len(wanted),
        ),
        out_shape=[shape(SIDE, cuts * depth, width)] * len(wanted),
        cost_estimate=FREE,
        compiler_params=limit(8),
        name="combine",
    )(coords, *operands, *after)


def first_kernel(coords_ref, up_even, up_odd, down_even, down_odd, after_ref, up_ref, down_ref):
    for out_ref, refs in ((up_ref, (up_even, up_odd)), (down_ref, (down_even, down_odd))):
        for index, ref in enumerate(refs):
            out_ref[index] = ref[0, 0, 0].astype(jnp.float32)


def first_blocks(blocks, coords, after):
    depth, width = blocks.shape[3:]
    specs = []
    for half in (0, 1):
        for odd in (0, 1):

            def where(k, s, half=half, odd=odd):
                there, core, spot = s[2], s[2 * SIDE], 2 * k + odd
                return there * (1 - core) + spot * core, there * core + spot * (1 - core), half, 0, 0

            specs.append(pl.BlockSpec((1, 1, 1, depth, width), where))
    whole = pl.BlockSpec((2, depth, width), lambda k, s: (k, 0, 0))
    return pl.pallas_call(
        first_kernel,
        grid_spec=pltpu.PrefetchScalarGridSpec(
            num_scalar_prefetch=1, grid=(SIDE // 2,), in_specs=specs + [ANY], out_specs=[whole] * 2
        ),
        out_shape=[shape(SIDE, depth, width)] * 2,
        cost_estimate=FREE,
        compiler_params=limit(10),
        name="first_blocks",
    )(coords, *[blocks] * 4, after)


def turn_first_kernel(coords_ref, held_up, came_up, held_down, came_down, up, down):
    there = coords_ref[SIDE + 2]
    up[...] = held_up[there] + came_up[there]
    down[...] = held_down[there] + came_down[there]


def turn_rest_kernel(coords_ref, held_up, came_up, held_down, came_down, up, down, kept_up, kept_down, own):
    depth = held_up.shape[1]
    there = [coords_ref[SIDE + spot] for spot in range(SIDE)]
    high = lambda spot: held_up[there[spot]] + came_up[there[spot]]
    low = lambda spot: held_down[there[spot]] + came_down[there[spot]]
    up[...] = low(1)
    down[...] = high(3)
    kept_up[...] = high(1)
    kept_down[...] = low(3)
    own[:depth, :] = high(0)
    own[depth:, :] = low(0)


def turn(coords, pairs, after):
    depth, width = pairs[0][0].shape[1:]
    part, terms = shape(depth, width), [*pairs[0], *pairs[1]]
    first = run(turn_first_kernel, [part] * 2, coords, terms, after, "turn_first")
    outs = [part] * 4 + [shape(2 * depth, width)]
    return [*first, *run(turn_rest_kernel, outs, coords, terms, first[0], "turn_rest")]


def ring_add_kernel(mine_up, came_up, mine_down, came_down, up_ref, down_ref):
    up_ref[...] = mine_up[...] + came_up[...]
    down_ref[...] = mine_down[...] + came_down[...]


def pieces_of(values):
    high = values.astype(jnp.bfloat16)
    rest = values - high.astype(jnp.float32)
    middle = rest.astype(jnp.bfloat16)
    low = (rest - middle.astype(jnp.float32)).astype(jnp.bfloat16)
    return high, middle, low


def stacked(values, order):
    pieces = pieces_of(values)
    return [pieces[index] for index in order]


LEFT_ORDER, RIGHT_ORDER = (0, 0, 1, 1, 0, 2), (0, 1, 0, 1, 2, 0)


def left_kernel(
    scalar_ref, partial_ref, basis_ref, error_ref, after_ref, keep_ref, send_ref, copy_ref, pieces, total
):
    step = pl.program_id(0)
    count, own = basis_ref.shape[0], error_ref.shape[0]
    size = partial_ref.shape[0]
    half = count // 2
    across = (((1,), (1,)), ((), ()))

    @pl.when(step == 0)
    def _():
        for index, piece in enumerate(pieces_of(basis_ref[...])):
            pieces[index * count : (index + 1) * count, :] = piece

    copy_ref[...] = partial_ref[...]
    three = lax.dot_general(pieces[...], partial_ref[...], across, preferred_element_type=jnp.float32)
    total[:, span(step, size)] = three[:count] + (three[count : 2 * count] + three[2 * count :])

    @pl.when(step == pl.num_programs(0) - 1)
    def _():
        shard, core = scalar_ref[0], scalar_ref[1]
        terms = jnp.concatenate(pieces_of(error_ref[...]), axis=0)
        nine = lax.dot_general(pieces[...], terms, across, preferred_element_type=jnp.float32)
        block = lambda i, j: nine[i * count : (i + 1) * count, j * own : (j + 1) * own]
        kept = block(0, 0) + ((block(0, 1) + block(1, 0)) + (block(1, 1) + (block(0, 2) + block(2, 0))))
        wide = jnp.concatenate([kept] * (LANES // own), axis=1)
        lane = lax.broadcasted_iota(jnp.int32, wide.shape, 1)
        there = span(shard // (LANES // own), LANES)
        total[:, there] += jnp.where(lane // own == shard % (LANES // own), wide, 0.0)
        keep_ref[...] = total[span(core, half), :]
        send_ref[...] = total[span(1 - core, half), :]


def left_terms(scalars, partial, basis, error, after):
    rows, width = partial.shape
    count = basis.shape[0]
    size = rows // SIDE
    fixed = lambda k: (0, 0)
    return pl.pallas_call(
        left_kernel,
        grid=(SIDE,),
        in_specs=[
            SCALARS,
            pl.BlockSpec((size, width), lambda k: (k, 0)),
            pl.BlockSpec(basis.shape, fixed, pipeline_mode=ONCE),
            pl.BlockSpec(error.shape, fixed, pipeline_mode=ONCE),
            ANY,
        ],
        out_specs=[pl.BlockSpec((count // 2, rows), fixed)] * 2
        + [pl.BlockSpec((size, width), lambda k: (k, 0))],
        out_shape=[shape(count // 2, rows)] * 2 + [shape(rows, width, dtype=partial.dtype)],
        scratch_shapes=[pltpu.VMEM((3 * count, width), jnp.bfloat16), pltpu.VMEM((count, rows), jnp.float32)],
        cost_estimate=FREE,
        compiler_params=limit(16),
        name="left_terms",
    )(scalars, partial, basis, error, after)


def ordered(core, mine, other):
    return jnp.where(core == 0, mine, other), jnp.where(core == 0, other, mine)


def orthonormal_kernel(scalar_ref, mine_ref, other_ref, out_ref, pieces_ref):
    mat = jnp.concatenate(ordered(1 - scalar_ref[1], mine_ref[...], other_ref[...]), axis=0)
    count = mat.shape[0]
    size = SUBLANES
    groups = [mat[start : start + size, :] for start in range(0, count, size)]
    order = lax.broadcasted_iota(jnp.int32, (size, 1), 0)
    for index in range(count):
        group, spot = index // size, index % size
        column = groups[group][spot : spot + 1, :]
        products = [jnp.sum(later * column, axis=1, keepdims=True) for later in groups[group:]]
        own_norm = products[0][spot : spot + 1, :]
        weights = [product / own_norm for product in products]
        weights[0] = jnp.where(order > spot, weights[0], 0.0)
        scaled = column / jnp.sqrt(own_norm)
        groups[group:] = [later - weight * column for later, weight in zip(groups[group:], weights)]
        groups[group] = jnp.where(order == spot, scaled, groups[group])
    mat = jnp.concatenate(groups, axis=0)
    out_ref[...] = mat
    for index, piece in enumerate(pieces_of(mat)):
        pieces_ref[index * count : (index + 1) * count, :] = piece


def own_rows(phat, shard, own):
    parts = [phat[:, start : start + own] for start in range(0, LANES, own)]
    chosen = parts[0]
    for index, part in enumerate(parts[1:], 1):
        chosen = jnp.where(shard % (LANES // own) == index, part, chosen)
    return chosen


def right_kernel(scalar_ref, pieces_ref, partial_ref, phat_ref, error_ref, after_ref, keep_ref, send_ref, total):
    step = pl.program_id(0)
    count, own = phat_ref.shape[0], error_ref.shape[0]
    width = partial_ref.shape[1]
    half = count // 2
    three = jnp.dot(pieces_ref[...], partial_ref[...], preferred_element_type=jnp.float32)
    terms = three[:count] + (three[count : 2 * count] + three[2 * count :])

    @pl.when(step == 0)
    def _():
        shard = scalar_ref[0]
        mine = own_rows(phat_ref[:, span(shard // (LANES // own), LANES)], shard, own)
        total[:, :width] = terms + jnp.dot(
            mine, error_ref[...], precision=HIGHEST, preferred_element_type=jnp.float32
        )
        total[:, width:] = jnp.zeros((count, total.shape[1] - width), jnp.float32)

    @pl.when(step > 0)
    def _():
        total[:, :width] += terms

    @pl.when(step == pl.num_programs(0) - 1)
    def _():
        core = scalar_ref[1]
        keep_ref[...] = total[span(core, half), :]
        send_ref[...] = total[span(1 - core, half), :]


def right_terms(scalars, pieces, partial, phat, error, after):
    rows, width = partial.shape
    count = phat.shape[0]
    padded = -(-width // (LANES * SIDE)) * LANES * SIDE
    size = rows // SIDE
    fixed = lambda k: (0, 0)
    return pl.pallas_call(
        right_kernel,
        grid=(SIDE,),
        in_specs=[
            SCALARS,
            pl.BlockSpec((3 * count, size), lambda k: (0, k)),
            pl.BlockSpec((size, width), lambda k: (k, 0)),
            pl.BlockSpec(phat.shape, fixed, pipeline_mode=ONCE),
            pl.BlockSpec(error.shape, fixed, pipeline_mode=ONCE),
            ANY,
        ],
        out_specs=[pl.BlockSpec((count // 2, padded), fixed)] * 2,
        out_shape=[shape(count // 2, padded)] * 2,
        scratch_shapes=[pltpu.VMEM((count, padded), jnp.float32)],
        cost_estimate=FREE,
        compiler_params=limit(12),
        name="right_terms",
    )(scalars, pieces, partial, phat, error, after)


def gate(arrays, after):
    return pl.pallas_call(
        lambda *refs: None,
        in_specs=[ANY] * (len(arrays) + len(after)),
        out_specs=[ANY] * len(arrays),
        out_shape=[shape(*array.shape) for array in arrays],
        input_output_aliases={index: index for index in range(len(arrays))},
        cost_estimate=FREE,
        compiler_params=limit(1),
        name="gate",
    )(*arrays, *after)


def add_kernel(*refs):
    terms = [ref[...] for ref in refs[:-1]]
    refs[-1][...] = sum(terms[1:], terms[0])


def add(terms, after):
    return run(add_kernel, [shape(*terms[0].shape)], None, terms, after, "add", room=1)[0]


def add_four_kernel(a_ref, b_ref, c_ref, d_ref, out_ref):
    out_ref[...] = (a_ref[...] + b_ref[...]) + (c_ref[...] + d_ref[...])


def sum_four(values, along, after):
    return sum_came(values, [along(values, step) for step in (2, 1, -1)], after)


def sum_came(values, came, after):
    outs = [shape(*values.shape)]
    return run(add_four_kernel, outs, None, [values, *came], after, "add_four", room=1)[0]


def sum_pairs(values, pairs, after):
    for mask in (1, 3):
        values = after = add([values, pairs(values, mask)], after)
    return values


def add_cut_kernel(scalar_ref, a_ref, b_ref, *out_refs):
    x, size = scalar_ref[2], out_refs[0].shape[1]
    for index, out_ref in enumerate(out_refs):
        there = span(lax.rem(x + index, SIDE), size)
        out_ref[...] = a_ref[:, there] + b_ref[:, there]


def scatter_x(scalars, keep, came, after):
    outs = [shape(keep.shape[0], keep.shape[1] // SIDE)] * SIDE
    parts = run(add_cut_kernel, outs, scalars, [keep, came], after, "add_cut")
    came = [along_x(parts[2], 2), along_x(parts[1], 1), along_x(parts[3], -1)]
    return run(add_four_kernel, outs[:1], None, [parts[0], *came], parts[0], "add_four", room=1)[0]


def join_two_kernel(a_ref, b_ref, out_ref):
    size = a_ref.shape[1]
    out_ref[:, :size] = a_ref[...]
    out_ref[:, size:] = b_ref[...]


def join_four_kernel(scalar_ref, mine_ref, came_ref, out_ref):
    x, size = scalar_ref[2], mine_ref.shape[1] // 2
    for ref, masks in ((mine_ref, (0, 3)), (came_ref, (1, 2))):
        for index, mask in enumerate(masks):
            out_ref[:, span(x ^ mask, size)] = ref[:, index * size : (index + 1) * size]


def product(left, right, replicas):
    total = lax.dot_general(
        jnp.concatenate(stacked(left, LEFT_ORDER), axis=0),
        jnp.concatenate(stacked(right, RIGHT_ORDER), axis=0),
        (((0,), (0,)), ((), ())),
        preferred_element_type=jnp.float32,
    )
    return total * (1.0 / replicas)


def half_product(replicas, scalar_ref, half, values_ref, phat_ref, own, width):
    shard, count = scalar_ref[0], values_ref.shape[0]
    mine = own_rows(phat_ref[span(half, count), span(shard // (LANES // own), LANES)], shard, own)
    return product(mine, values_ref[:, :width], replicas)


def nearly_kernel(replicas, scalar_ref, mine_ref, phat_ref, error_ref, kept_ref, up_ref, down_ref, *out_refs):
    half_ref, rest_ref = out_refs
    own, width = error_ref.shape
    approx = half_product(replicas, scalar_ref, scalar_ref[1], mine_ref, phat_ref, own, width)
    half_ref[...] = approx
    depth = own // 2
    for rows, came_ref in ((slice(0, depth), down_ref), (slice(depth, own), up_ref)):
        rest_ref[rows, :] = (error_ref[rows, :] + (kept_ref[rows, :] + came_ref[...])) - approx[rows, :]


def finish_kernel(
    replicas, scalar_ref, mine_ref, other_ref, phat_ref, half_ref, rest_ref, up_ref, down_ref, *out_refs
):
    grad_ref, next_ref, basis_ref = out_refs
    core = scalar_ref[1]
    own, width = rest_ref.shape
    count, depth = mine_ref.shape[0], own // 2
    basis_ref[span(core, count), :] = mine_ref[:, :width] * (1.0 / replicas)
    basis_ref[span(1 - core, count), :] = other_ref[:, :width] * (1.0 / replicas)
    approx = half_product(replicas, scalar_ref, 1 - core, other_ref, phat_ref, own, width)
    grad_ref[...] = (half_ref[...] + approx).astype(jnp.bfloat16)
    for rows, came_ref in ((slice(0, depth), up_ref), (slice(depth, own), down_ref)):
        next_ref[rows, :] = (rest_ref[rows, :] + came_ref[...]) - approx[rows, :]


def shards(partials, error, basis):
    replicas = lax.axis_size("dp")
    dp, shard = lax.axis_index("dp"), lax.axis_index("shard")
    x, core = dp // 2, dp % 2
    partial, error, basis = partials[0, 0], error[0], basis.T
    rows, width = partial.shape
    own, count = error.shape[0], basis.shape[0]
    depth = own // 2
    scalars = jnp.stack([shard, core, x]).astype(jnp.int32)
    z, y = shard // SIDE, shard % SIDE
    first, second = jnp.where(core == 0, z, y), jnp.where(core == 0, y, z)
    near = jnp.arange(SIDE)
    coords = jnp.concatenate([(first + near) % SIDE, (second + near) % SIDE, core[None]])
    coords = coords.astype(jnp.int32)
    large = in_hbm(partial.reshape(SIDE, SIDE, 2, own // 2, width))

    sent1 = first_blocks(large, coords, scalars)
    came1 = [along_first(sent1[0], 1), along_first(sent1[1], -1)]
    keep, send, partial = left_terms(scalars, in_hbm(partial), basis, error, sent1[0])
    blocks = partial.reshape(SIDE, SIDE, 4, own // 4, width)
    part = add([keep, other_core(send)], keep)
    sent2 = combine(blocks, coords, [(1, 1, []), (3, 0, [])], part)
    part = sum_four(part, along_x, sent2[0])
    sent2 = gate(sent2, [part])
    came2 = [along_first(sent2[0], 1), along_first(sent2[1], -1)]
    part = sum_pairs(part, pair_second, sent2[0])
    sent3 = combine(blocks, coords, [(1, 0, [came1[0]]), (3, 1, [came1[1]])], part)
    (part,) = gate([other_core(part)], [sent3[0]])
    part = sum_four(part, along_second, part)
    sent3 = gate(sent3, [part])
    came3 = [along_first(sent3[0], 1), along_first(sent3[1], -1)]
    phat, pieces = run(
        orthonormal_kernel,
        [shape(count, rows), shape(3 * count, rows, dtype=jnp.bfloat16)],
        scalars,
        [part, other_core(part)],
        sent3[0],
        "orthonormal",
    )
    keep, send = right_terms(scalars, pieces, partial, phat, error, phat)
    held = combine(blocks, coords, [(0, 0, [came2[1]]), (0, 1, [came2[0]])], send)
    part = scatter_x(scalars, keep, other_core(send), held[0])
    part = sum_four(part, along_second, part)
    came = [along_first(part, step) for step in (2, 1, -1)]
    up, down, up_local, down_local, kept_up, kept_down, kept = turn(
        coords, [(held[0], came3[0]), (held[1], came3[1])], came
    )
    came4 = [along_second(up, 1), along_second(down, -1)]
    came5 = [along_second(up_local, 1), along_second(down_local, -1)]
    part = sum_came(part, came, kept)
    pair = run(join_two_kernel, [shape(count // 2, 2 * part.shape[1])], None, [part, pair_x(part, 3)], part, "join", room=1)[0]
    sent6 = run(
        ring_add_kernel,
        [shape(own // 2, width)] * 2,
        None,
        [kept_up, came4[0], kept_down, came4[1]],
        pair,
        "ring_add",
    )
    came6 = [along_second(sent6[0], 1), along_second(sent6[1], -1)]
    outs = [shape(count // 2, 2 * pair.shape[1])]
    part = run(join_four_kernel, outs, scalars, [pair, pair_x(pair, 1)], sent6[0], "join")[0]
    half, rest = run(
        functools.partial(nearly_kernel, replicas),
        [shape(own, width)] * 2,
        scalars,
        [part, phat, error, kept, *came5],
        part,
        "nearly",
    )
    grad, following, right = run(
        functools.partial(finish_kernel, replicas),
        [shape(own, width, dtype=jnp.bfloat16), shape(own, width), shape(count, width)],
        scalars,
        [part, other_core(part), phat, half, rest, *came6],
        rest,
        "finish",
    )
    return grad, following[None], right.T


def solution(mesh):
    return jax.shard_map(
        shards,
        mesh=mesh,
        in_specs=(P("dp", "shard", None, None), P("dp", "shard", None), P()),
        out_specs=(P("shard", None), P("dp", "shard", None), P()),
        check_vma=False,
    )
```

```python
import functools

import jax
import jax.numpy as jnp
from jax import lax
from jax.experimental import pallas as pl
from jax.experimental.pallas import tpu as pltpu
from jax.sharding import PartitionSpec as P

BOTH = ("dp", "shard")
SIDE = 4
LANES = 128
SUBLANES = 8
HIGHEST = lax.Precision.HIGHEST
FREE = pl.CostEstimate(flops=0, bytes_accessed=0, transcendentals=0)
ANY = pl.BlockSpec(memory_space=pl.ANY)
ONCE = pl.Buffered(1)
WHOLE = pl.BlockSpec(memory_space=pltpu.VMEM)
SCALARS = pl.BlockSpec(memory_space=pltpu.SMEM)


def limit(mebibytes):
    return pltpu.CompilerParams(vmem_limit_bytes=mebibytes << 20)


def place(x, c, z, y):
    return ((x % SIDE) * 2 + c % 2) * SIDE * SIDE + (z % SIDE) * SIDE + y % SIDE


def moved(values, route):
    spots = [
        (x, c, z, y)
        for x in range(SIDE)
        for c in range(2)
        for z in range(SIDE)
        for y in range(SIDE)
    ]
    return lax.ppermute(values, BOTH, [(place(*spot), place(*route(*spot))) for spot in spots])


def other_core(values):
    return moved(values, lambda x, c, z, y: (x, 1 - c, z, y))


def along_x(values, step):
    return moved(values, lambda x, c, z, y: (x + step, c, z, y))


def along_first(values, step):
    return moved(values, lambda x, c, z, y: (x, c, z + step * (1 - c), y + step * c))


def along_second(values, step):
    return moved(values, lambda x, c, z, y: (x, c, z + step * c, y + step * (1 - c)))


def pair_x(values, mask):
    return moved(values, lambda x, c, z, y: (x ^ mask, c, z, y))


def pair_second(values, mask):
    return moved(values, lambda x, c, z, y: (x, c, z ^ (mask * c), y ^ (mask * (1 - c))))


def shape(*dims, dtype=jnp.float32):
    return jax.ShapeDtypeStruct(dims, dtype)


def run(kernel, outs, scalars, operands, after, name, room=8, scratch=()):
    after = after if isinstance(after, list) else [after]

    scalars = [] if scalars is None else [scalars]
    count = len(scalars) + len(operands)

    def body(*refs):
        kernel(*refs[:count], *refs[count + len(after) :])

    return pl.pallas_call(
        body,
        in_specs=[SCALARS] * len(scalars) + [WHOLE] * len(operands) + [ANY] * len(after),
        out_specs=[WHOLE] * len(outs),
        out_shape=outs,
        scratch_shapes=list(scratch),
        cost_estimate=FREE,
        compiler_params=limit(room),
        name=name,
    )(*scalars, *operands, *after)


def in_hbm(values):
    return pltpu.with_memory_space_constraint(values, pltpu.HBM)


def span(index, size):
    return pl.ds(pl.multiple_of(index * size, size), size)


def combine_kernel(arity, coords_ref, *refs):
    inputs, outputs = refs[: sum(arity)], refs[-len(arity) :]
    start = 0
    for count, out_ref in zip(arity, outputs):
        own, *came = [ref[...] for ref in inputs[start : start + count]]
        total = own[0, 0, 0].astype(jnp.float32)
        for block in came:
            total = total + block[0]
        out_ref[0] = total
        start += count


def combine(blocks, coords, wanted, after):
    after = after if isinstance(after, list) else [after]
    depth, width = blocks.shape[3:]
    cuts = blocks.shape[2] // 2
    arity, operands, specs = [], [], []
    whole = pl.BlockSpec((1, depth, width), lambda k, i, s: (k, i, 0))
    for owner, half, came in wanted:

        def where(k, i, s, owner=owner, half=half):
            there, core = s[owner], s[2 * SIDE]
            return there * (1 - core) + k * core, there * core + k * (1 - core), half * cuts + i, 0, 0

        operands += [blocks, *came]
        specs += [pl.BlockSpec((1, 1, 1, depth, width), where)] + [whole] * len(came)
        arity.append(1 + len(came))
    return pl.pallas_call(
        functools.partial(combine_kernel, arity),
        grid_spec=pltpu.PrefetchScalarGridSpec(
            num_scalar_prefetch=1,
            grid=(SIDE, cuts),
            in_specs=specs + [ANY] * len(after),
            out_specs=[whole] * len(wanted),
        ),
        out_shape=[shape(SIDE, cuts * depth, width)] * len(wanted),
        cost_estimate=FREE,
        compiler_params=limit(8),
        name="combine",
    )(coords, *operands, *after)


def first_kernel(coords_ref, up_even, up_odd, down_even, down_odd, after_ref, up_ref, down_ref):
    for out_ref, refs in ((up_ref, (up_even, up_odd)), (down_ref, (down_even, down_odd))):
        for index, ref in enumerate(refs):
            out_ref[index] = ref[0, 0, 0].astype(jnp.float32)


def first_blocks(blocks, coords, after):
    depth, width = blocks.shape[3:]
    specs = []
    for half in (0, 1):
        for odd in (0, 1):

            def where(k, s, half=half, odd=odd):
                there, core, spot = s[2], s[2 * SIDE], 2 * k + odd
                return there * (1 - core) + spot * core, there * core + spot * (1 - core), half, 0, 0

            specs.append(pl.BlockSpec((1, 1, 1, depth, width), where))
    whole = pl.BlockSpec((2, depth, width), lambda k, s: (k, 0, 0))
    return pl.pallas_call(
        first_kernel,
        grid_spec=pltpu.PrefetchScalarGridSpec(
            num_scalar_prefetch=1, grid=(SIDE // 2,), in_specs=specs + [ANY], out_specs=[whole] * 2
        ),
        out_shape=[shape(SIDE, depth, width)] * 2,
        cost_estimate=FREE,
        compiler_params=limit(10),
        name="first_blocks",
    )(coords, *[blocks] * 4, after)


def turn_first_kernel(coords_ref, held_up, came_up, held_down, came_down, up, down):
    there = coords_ref[SIDE + 2]
    up[...] = held_up[there] + came_up[there]
    down[...] = held_down[there] + came_down[there]


def turn_rest_kernel(coords_ref, held_up, came_up, held_down, came_down, up, down, kept_up, kept_down, own):
    depth = held_up.shape[1]
    there = [coords_ref[SIDE + spot] for spot in range(SIDE)]
    high = lambda spot: held_up[there[spot]] + came_up[there[spot]]
    low = lambda spot: held_down[there[spot]] + came_down[there[spot]]
    up[...] = low(1)
    down[...] = high(3)
    kept_up[...] = high(1)
    kept_down[...] = low(3)
    own[:depth, :] = high(0)
    own[depth:, :] = low(0)


def turn(coords, pairs, after):
    depth, width = pairs[0][0].shape[1:]
    part, terms = shape(depth, width), [*pairs[0], *pairs[1]]
    first = run(turn_first_kernel, [part] * 2, coords, terms, after, "turn_first")
    outs = [part] * 4 + [shape(2 * depth, width)]
    return [*first, *run(turn_rest_kernel, outs, coords, terms, first[0], "turn_rest")]


def ring_add_kernel(mine_up, came_up, mine_down, came_down, up_ref, down_ref):
    up_ref[...] = mine_up[...] + came_up[...]
    down_ref[...] = mine_down[...] + came_down[...]


def pieces_of(values):
    high = values.astype(jnp.bfloat16)
    rest = values - high.astype(jnp.float32)
    middle = rest.astype(jnp.bfloat16)
    low = (rest - middle.astype(jnp.float32)).astype(jnp.bfloat16)
    return high, middle, low


def stacked(values, order):
    pieces = pieces_of(values)
    return [pieces[index] for index in order]


LEFT_ORDER, RIGHT_ORDER = (0, 0, 1, 1, 0, 2), (0, 1, 0, 1, 2, 0)


def left_kernel(
    scalar_ref, partial_ref, basis_ref, error_ref, after_ref, keep_ref, send_ref, copy_ref, pieces, total
):
    step = pl.program_id(0)
    count, own = basis_ref.shape[0], error_ref.shape[0]
    size = partial_ref.shape[0]
    half = count // 2
    across = (((1,), (1,)), ((), ()))

    @pl.when(step == 0)
    def _():
        for index, piece in enumerate(pieces_of(basis_ref[...])):
            pieces[index * count : (index + 1) * count, :] = piece

    copy_ref[...] = partial_ref[...]
    three = lax.dot_general(pieces[...], partial_ref[...], across, preferred_element_type=jnp.float32)
    total[:, span(step, size)] = three[:count] + (three[count : 2 * count] + three[2 * count :])

    @pl.when(step == pl.num_programs(0) - 1)
    def _():
        shard, core = scalar_ref[0], scalar_ref[1]
        terms = jnp.concatenate(pieces_of(error_ref[...]), axis=0)
        nine = lax.dot_general(pieces[...], terms, across, preferred_element_type=jnp.float32)
        block = lambda i, j: nine[i * count : (i + 1) * count, j * own : (j + 1) * own]
        kept = block(0, 0) + ((block(0, 1) + block(1, 0)) + (block(1, 1) + (block(0, 2) + block(2, 0))))
        wide = jnp.concatenate([kept] * (LANES // own), axis=1)
        lane = lax.broadcasted_iota(jnp.int32, wide.shape, 1)
        there = span(shard // (LANES // own), LANES)
        total[:, there] += jnp.where(lane // own == shard % (LANES // own), wide, 0.0)
        keep_ref[...] = total[span(core, half), :]
        send_ref[...] = total[span(1 - core, half), :]


def left_terms(scalars, partial, basis, error, after):
    rows, width = partial.shape
    count = basis.shape[0]
    size = rows // SIDE
    fixed = lambda k: (0, 0)
    return pl.pallas_call(
        left_kernel,
        grid=(SIDE,),
        in_specs=[
            SCALARS,
            pl.BlockSpec((size, width), lambda k: (k, 0)),
            pl.BlockSpec(basis.shape, fixed, pipeline_mode=ONCE),
            pl.BlockSpec(error.shape, fixed, pipeline_mode=ONCE),
            ANY,
        ],
        out_specs=[pl.BlockSpec((count // 2, rows), fixed)] * 2
        + [pl.BlockSpec((size, width), lambda k: (k, 0))],
        out_shape=[shape(count // 2, rows)] * 2 + [shape(rows, width, dtype=partial.dtype)],
        scratch_shapes=[pltpu.VMEM((3 * count, width), jnp.bfloat16), pltpu.VMEM((count, rows), jnp.float32)],
        cost_estimate=FREE,
        compiler_params=limit(16),
        name="left_terms",
    )(scalars, partial, basis, error, after)


def ordered(core, mine, other):
    return jnp.where(core == 0, mine, other), jnp.where(core == 0, other, mine)


def orthonormal_kernel(scalar_ref, mine_ref, other_ref, out_ref, pieces_ref):
    mat = jnp.concatenate(ordered(1 - scalar_ref[1], mine_ref[...], other_ref[...]), axis=0)
    count = mat.shape[0]
    size = SUBLANES
    groups = [mat[start : start + size, :] for start in range(0, count, size)]
    order = lax.broadcasted_iota(jnp.int32, (size, 1), 0)
    for index in range(count):
        group, spot = index // size, index % size
        column = groups[group][spot : spot + 1, :]
        products = [jnp.sum(later * column, axis=1, keepdims=True) for later in groups[group:]]
        own_norm = products[0][spot : spot + 1, :]
        weights = [product / own_norm for product in products]
        weights[0] = jnp.where(order > spot, weights[0], 0.0)
        scaled = column / jnp.sqrt(own_norm)
        groups[group:] = [later - weight * column for later, weight in zip(groups[group:], weights)]
        groups[group] = jnp.where(order == spot, scaled, groups[group])
    mat = jnp.concatenate(groups, axis=0)
    out_ref[...] = mat
    for index, piece in enumerate(pieces_of(mat)):
        pieces_ref[index * count : (index + 1) * count, :] = piece


def own_rows(phat, shard, own):
    parts = [phat[:, start : start + own] for start in range(0, LANES, own)]
    chosen = parts[0]
    for index, part in enumerate(parts[1:], 1):
        chosen = jnp.where(shard % (LANES // own) == index, part, chosen)
    return chosen


def right_kernel(scalar_ref, pieces_ref, partial_ref, phat_ref, error_ref, after_ref, keep_ref, send_ref, total):
    step = pl.program_id(0)
    count, own = phat_ref.shape[0], error_ref.shape[0]
    width = partial_ref.shape[1]
    half = count // 2
    three = jnp.dot(pieces_ref[...], partial_ref[...], preferred_element_type=jnp.float32)
    terms = three[:count] + (three[count : 2 * count] + three[2 * count :])

    @pl.when(step == 0)
    def _():
        shard = scalar_ref[0]
        mine = own_rows(phat_ref[:, span(shard // (LANES // own), LANES)], shard, own)
        total[:, :width] = terms + jnp.dot(
            mine, error_ref[...], precision=HIGHEST, preferred_element_type=jnp.float32
        )
        total[:, width:] = jnp.zeros((count, total.shape[1] - width), jnp.float32)

    @pl.when(step > 0)
    def _():
        total[:, :width] += terms

    @pl.when(step == pl.num_programs(0) - 1)
    def _():
        core = scalar_ref[1]
        keep_ref[...] = total[span(core, half), :]
        send_ref[...] = total[span(1 - core, half), :]


def right_terms(scalars, pieces, partial, phat, error, after):
    rows, width = partial.shape
    count = phat.shape[0]
    padded = -(-width // (LANES * SIDE)) * LANES * SIDE
    size = rows // SIDE
    fixed = lambda k: (0, 0)
    return pl.pallas_call(
        right_kernel,
        grid=(SIDE,),
        in_specs=[
            SCALARS,
            pl.BlockSpec((3 * count, size), lambda k: (0, k)),
            pl.BlockSpec((size, width), lambda k: (k, 0)),
            pl.BlockSpec(phat.shape, fixed, pipeline_mode=ONCE),
            pl.BlockSpec(error.shape, fixed, pipeline_mode=ONCE),
            ANY,
        ],
        out_specs=[pl.BlockSpec((count // 2, padded), fixed)] * 2,
        out_shape=[shape(count // 2, padded)] * 2,
        scratch_shapes=[pltpu.VMEM((count, padded), jnp.float32)],
        cost_estimate=FREE,
        compiler_params=limit(12),
        name="right_terms",
    )(scalars, pieces, partial, phat, error, after)


def gate(arrays, after):
    return pl.pallas_call(
        lambda *refs: None,
        in_specs=[ANY] * (len(arrays) + len(after)),
        out_specs=[ANY] * len(arrays),
        out_shape=[shape(*array.shape) for array in arrays],
        input_output_aliases={index: index for index in range(len(arrays))},
        cost_estimate=FREE,
        compiler_params=limit(1),
        name="gate",
    )(*arrays, *after)


def add_kernel(*refs):
    terms = [ref[...] for ref in refs[:-1]]
    refs[-1][...] = sum(terms[1:], terms[0])


def add(terms, after):
    return run(add_kernel, [shape(*terms[0].shape)], None, terms, after, "add", room=1)[0]


def add_four_kernel(a_ref, b_ref, c_ref, d_ref, out_ref):
    out_ref[...] = (a_ref[...] + b_ref[...]) + (c_ref[...] + d_ref[...])


def sum_four(values, along, after):
    return sum_came(values, [along(values, step) for step in (2, 1, -1)], after)


def sum_came(values, came, after):
    outs = [shape(*values.shape)]
    return run(add_four_kernel, outs, None, [values, *came], after, "add_four", room=1)[0]


def sum_pairs(values, pairs, after):
    for mask in (1, 3):
        values = after = add([values, pairs(values, mask)], after)
    return values


def add_cut_kernel(scalar_ref, a_ref, b_ref, *out_refs):
    x, size = scalar_ref[2], out_refs[0].shape[1]
    for index, out_ref in enumerate(out_refs):
        there = span(lax.rem(x + index, SIDE), size)
        out_ref[...] = a_ref[:, there] + b_ref[:, there]


def scatter_x(scalars, keep, came, after):
    outs = [shape(keep.shape[0], keep.shape[1] // SIDE)] * SIDE
    parts = run(add_cut_kernel, outs, scalars, [keep, came], after, "add_cut")
    came = [along_x(parts[2], 2), along_x(parts[1], 1), along_x(parts[3], -1)]
    return run(add_four_kernel, outs[:1], None, [parts[0], *came], parts[0], "add_four", room=1)[0]


def join_two_kernel(a_ref, b_ref, out_ref):
    size = a_ref.shape[1]
    out_ref[:, :size] = a_ref[...]
    out_ref[:, size:] = b_ref[...]


def join_four_kernel(scalar_ref, mine_ref, came_ref, out_ref):
    x, size = scalar_ref[2], mine_ref.shape[1] // 2
    for ref, masks in ((mine_ref, (0, 3)), (came_ref, (1, 2))):
        for index, mask in enumerate(masks):
            out_ref[:, span(x ^ mask, size)] = ref[:, index * size : (index + 1) * size]


def product(left, right, replicas):
    total = lax.dot_general(
        jnp.concatenate(stacked(left, LEFT_ORDER), axis=0),
        jnp.concatenate(stacked(right, RIGHT_ORDER), axis=0),
        (((0,), (0,)), ((), ())),
        preferred_element_type=jnp.float32,
    )
    return total * (1.0 / replicas)


def half_product(replicas, scalar_ref, half, values_ref, phat_ref, own, width):
    shard, count = scalar_ref[0], values_ref.shape[0]
    mine = own_rows(phat_ref[span(half, count), span(shard // (LANES // own), LANES)], shard, own)
    return product(mine, values_ref[:, :width], replicas)


def nearly_kernel(replicas, scalar_ref, mine_ref, phat_ref, error_ref, kept_ref, up_ref, down_ref, *out_refs):
    half_ref, rest_ref = out_refs
    own, width = error_ref.shape
    approx = half_product(replicas, scalar_ref, scalar_ref[1], mine_ref, phat_ref, own, width)
    half_ref[...] = approx
    depth = own // 2
    for rows, came_ref in ((slice(0, depth), down_ref), (slice(depth, own), up_ref)):
        rest_ref[rows, :] = (error_ref[rows, :] + (kept_ref[rows, :] + came_ref[...])) - approx[rows, :]


def finish_kernel(replicas, scalar_ref, mine_ref, other_ref, phat_ref, half_ref, rest_ref, *refs):
    up_ref, down_ref, grad_out, next_out, basis_out, grad_ref, next_ref, basis_ref, sent = refs
    core = scalar_ref[1]
    own, width = rest_ref.shape
    count, depth = mine_ref.shape[0], own // 2
    basis_ref[span(core, count), :] = mine_ref[:, :width] * (1.0 / replicas)
    basis_ref[span(1 - core, count), :] = other_ref[:, :width] * (1.0 / replicas)
    copies = [pltpu.make_async_copy(basis_ref, basis_out, sent.at[0])]
    copies[-1].start()
    approx = half_product(replicas, scalar_ref, 1 - core, other_ref, phat_ref, own, width)
    for index, came_ref in enumerate((up_ref, down_ref)):
        rows = slice(index * depth, (index + 1) * depth)
        there = pl.ds(index * depth, depth)
        next_ref[rows, :] = (rest_ref[rows, :] + came_ref[...]) - approx[rows, :]
        copies.append(pltpu.make_async_copy(next_ref.at[there, :], next_out.at[there, :], sent.at[1 + index]))
        copies[-1].start()
    grad_ref[...] = (half_ref[...] + approx).astype(jnp.bfloat16)
    copies.append(pltpu.make_async_copy(grad_ref, grad_out, sent.at[3]))
    copies[-1].start()
    for copy in copies:
        copy.wait()


def finish(replicas, outs, scalars, operands):
    return pl.pallas_call(
        functools.partial(finish_kernel, replicas),
        in_specs=[SCALARS] + [WHOLE] * len(operands),
        out_specs=[ANY] * len(outs),
        out_shape=outs,
        scratch_shapes=[pltpu.VMEM(out.shape, out.dtype) for out in outs]
        + [pltpu.SemaphoreType.DMA((4,))],
        cost_estimate=FREE,
        compiler_params=limit(10),
        name="finish",
    )(scalars, *operands)


def shards(partials, error, basis):
    replicas = lax.axis_size("dp")
    dp, shard = lax.axis_index("dp"), lax.axis_index("shard")
    x, core = dp // 2, dp % 2
    partial, error, basis = partials[0, 0], error[0], basis.T
    rows, width = partial.shape
    own, count = error.shape[0], basis.shape[0]
    depth = own // 2
    scalars = jnp.stack([shard, core, x]).astype(jnp.int32)
    z, y = shard // SIDE, shard % SIDE
    first, second = jnp.where(core == 0, z, y), jnp.where(core == 0, y, z)
    near = jnp.arange(SIDE)
    coords = jnp.concatenate([(first + near) % SIDE, (second + near) % SIDE, core[None]])
    coords = coords.astype(jnp.int32)
    large = in_hbm(partial.reshape(SIDE, SIDE, 2, own // 2, width))

    sent1 = first_blocks(large, coords, scalars)
    came1 = [along_first(sent1[0], 1), along_first(sent1[1], -1)]
    keep, send, partial = left_terms(scalars, in_hbm(partial), basis, error, sent1[0])
    blocks = partial.reshape(SIDE, SIDE, 4, own // 4, width)
    part = add([keep, other_core(send)], keep)
    sent2 = combine(blocks, coords, [(1, 1, []), (3, 0, [])], part)
    part = sum_four(part, along_x, sent2[0])
    sent2 = gate(sent2, [part])
    came2 = [along_first(sent2[0], 1), along_first(sent2[1], -1)]
    part = sum_pairs(part, pair_second, sent2[0])
    sent3 = combine(blocks, coords, [(1, 0, [came1[0]]), (3, 1, [came1[1]])], part)
    (part,) = gate([other_core(part)], [sent3[0]])
    part = sum_four(part, along_second, part)
    sent3 = gate(sent3, [part])
    came3 = [along_first(sent3[0], 1), along_first(sent3[1], -1)]
    phat, pieces = run(
        orthonormal_kernel,
        [shape(count, rows), shape(3 * count, rows, dtype=jnp.bfloat16)],
        scalars,
        [part, other_core(part)],
        sent3[0],
        "orthonormal",
    )
    keep, send = right_terms(scalars, pieces, partial, phat, error, phat)
    held = combine(blocks, coords, [(0, 0, [came2[1]]), (0, 1, [came2[0]])], send)
    part = scatter_x(scalars, keep, other_core(send), held[0])
    part = sum_four(part, along_second, part)
    came = [along_first(part, step) for step in (2, 1, -1)]
    up, down, up_local, down_local, kept_up, kept_down, kept = turn(
        coords, [(held[0], came3[0]), (held[1], came3[1])], came
    )
    came4 = [along_second(up, 1), along_second(down, -1)]
    came5 = [along_second(up_local, 1), along_second(down_local, -1)]
    part = sum_came(part, came, up)
    pair = run(join_two_kernel, [shape(count // 2, 2 * part.shape[1])], None, [part, pair_x(part, 3)], part, "join", room=1)[0]
    sent6 = run(
        ring_add_kernel,
        [shape(own // 2, width)] * 2,
        None,
        [kept_up, came4[0], kept_down, came4[1]],
        pair,
        "ring_add",
    )
    came6 = [along_second(sent6[0], 1), along_second(sent6[1], -1)]
    outs = [shape(count // 2, 2 * pair.shape[1])]
    part = run(join_four_kernel, outs, scalars, [pair, pair_x(pair, 1)], sent6[0], "join")[0]
    half, rest = run(
        functools.partial(nearly_kernel, replicas),
        [shape(own, width)] * 2,
        scalars,
        [part, phat, error, kept, *came5],
        part,
        "nearly",
    )
    grad, following, right = finish(
        replicas,
        [shape(own, width, dtype=jnp.bfloat16), shape(own, width), shape(count, width)],
        scalars,
        [part, other_core(part), phat, half, rest, *came6],
    )
    return grad, following[None], right.T


def solution(mesh):
    return jax.shard_map(
        shards,
        mesh=mesh,
        in_specs=(P("dp", "shard", None, None), P("dp", "shard", None), P()),
        out_specs=(P("shard", None), P("dp", "shard", None), P()),
        check_vma=False,
    )
```

```python
import functools

import jax
import jax.numpy as jnp
from jax import lax
from jax.experimental import pallas as pl
from jax.experimental.pallas import tpu as pltpu
from jax.sharding import PartitionSpec as P

BOTH = ("dp", "shard")
SIDE = 4
LANES = 128
SUBLANES = 8
HIGHEST = lax.Precision.HIGHEST
FREE = pl.CostEstimate(flops=0, bytes_accessed=0, transcendentals=0)
ANY = pl.BlockSpec(memory_space=pl.ANY)
ONCE = pl.Buffered(1)
WHOLE = pl.BlockSpec(memory_space=pltpu.VMEM)
SCALARS = pl.BlockSpec(memory_space=pltpu.SMEM)


def limit(mebibytes):
    return pltpu.CompilerParams(vmem_limit_bytes=mebibytes << 20)


def place(x, c, z, y):
    return ((x % SIDE) * 2 + c % 2) * SIDE * SIDE + (z % SIDE) * SIDE + y % SIDE


def moved(values, route):
    spots = [
        (x, c, z, y)
        for x in range(SIDE)
        for c in range(2)
        for z in range(SIDE)
        for y in range(SIDE)
    ]
    return lax.ppermute(values, BOTH, [(place(*spot), place(*route(*spot))) for spot in spots])


def other_core(values):
    return moved(values, lambda x, c, z, y: (x, 1 - c, z, y))


def along_x(values, step):
    return moved(values, lambda x, c, z, y: (x + step, c, z, y))


def along_first(values, step):
    return moved(values, lambda x, c, z, y: (x, c, z + step * (1 - c), y + step * c))


def along_second(values, step):
    return moved(values, lambda x, c, z, y: (x, c, z + step * c, y + step * (1 - c)))


def pair_x(values, mask):
    return moved(values, lambda x, c, z, y: (x ^ mask, c, z, y))


def pair_second(values, mask):
    return moved(values, lambda x, c, z, y: (x, c, z ^ (mask * c), y ^ (mask * (1 - c))))


def shape(*dims, dtype=jnp.float32):
    return jax.ShapeDtypeStruct(dims, dtype)


def run(kernel, outs, scalars, operands, after, name, room=8, scratch=()):
    after = after if isinstance(after, list) else [after]

    scalars = [] if scalars is None else [scalars]
    count = len(scalars) + len(operands)

    def body(*refs):
        kernel(*refs[:count], *refs[count + len(after) :])

    return pl.pallas_call(
        body,
        in_specs=[SCALARS] * len(scalars) + [WHOLE] * len(operands) + [ANY] * len(after),
        out_specs=[WHOLE] * len(outs),
        out_shape=outs,
        scratch_shapes=list(scratch),
        cost_estimate=FREE,
        compiler_params=limit(room),
        name=name,
    )(*scalars, *operands, *after)


def in_hbm(values):
    return pltpu.with_memory_space_constraint(values, pltpu.HBM)


def span(index, size):
    return pl.ds(pl.multiple_of(index * size, size), size)


def combine_kernel(arity, coords_ref, *refs):
    inputs, outputs = refs[: sum(arity)], refs[-len(arity) :]
    start = 0
    for count, out_ref in zip(arity, outputs):
        own, *came = [ref[...] for ref in inputs[start : start + count]]
        total = own[0, 0, 0].astype(jnp.float32)
        for block in came:
            total = total + block[0]
        out_ref[0] = total
        start += count


def combine(blocks, coords, wanted, after):
    after = after if isinstance(after, list) else [after]
    depth, width = blocks.shape[3:]
    cuts = blocks.shape[2] // 2
    arity, operands, specs = [], [], []
    whole = pl.BlockSpec((1, depth, width), lambda k, i, s: (k, i, 0))
    for owner, half, came in wanted:

        def where(k, i, s, owner=owner, half=half):
            there, core = s[owner], s[2 * SIDE]
            return there * (1 - core) + k * core, there * core + k * (1 - core), half * cuts + i, 0, 0

        operands += [blocks, *came]
        specs += [pl.BlockSpec((1, 1, 1, depth, width), where)] + [whole] * len(came)
        arity.append(1 + len(came))
    return pl.pallas_call(
        functools.partial(combine_kernel, arity),
        grid_spec=pltpu.PrefetchScalarGridSpec(
            num_scalar_prefetch=1,
            grid=(SIDE, cuts),
            in_specs=specs + [ANY] * len(after),
            out_specs=[whole] * len(wanted),
        ),
        out_shape=[shape(SIDE, cuts * depth, width)] * len(wanted),
        cost_estimate=FREE,
        compiler_params=limit(8),
        name="combine",
    )(coords, *operands, *after)


def first_kernel(coords_ref, up_even, up_odd, down_even, down_odd, after_ref, up_ref, down_ref):
    for out_ref, refs in ((up_ref, (up_even, up_odd)), (down_ref, (down_even, down_odd))):
        for index, ref in enumerate(refs):
            out_ref[index] = ref[0, 0, 0].astype(jnp.float32)


def first_blocks(blocks, coords, after):
    depth, width = blocks.shape[3:]
    specs = []
    for half in (0, 1):
        for odd in (0, 1):

            def where(k, s, half=half, odd=odd):
                there, core, spot = s[2], s[2 * SIDE], 2 * k + odd
                return there * (1 - core) + spot * core, there * core + spot * (1 - core), half, 0, 0

            specs.append(pl.BlockSpec((1, 1, 1, depth, width), where))
    whole = pl.BlockSpec((2, depth, width), lambda k, s: (k, 0, 0))
    return pl.pallas_call(
        first_kernel,
        grid_spec=pltpu.PrefetchScalarGridSpec(
            num_scalar_prefetch=1, grid=(SIDE // 2,), in_specs=specs + [ANY], out_specs=[whole] * 2
        ),
        out_shape=[shape(SIDE, depth, width)] * 2,
        cost_estimate=FREE,
        compiler_params=limit(10),
        name="first_blocks",
    )(coords, *[blocks] * 4, after)


def turn_first_kernel(coords_ref, held_up, came_up, held_down, came_down, up, down):
    there = coords_ref[SIDE + 2]
    up[...] = held_up[there] + came_up[there]
    down[...] = held_down[there] + came_down[there]


def turn_rest_kernel(coords_ref, held_up, came_up, held_down, came_down, up, down, kept_up, kept_down, own):
    depth = held_up.shape[1]
    there = [coords_ref[SIDE + spot] for spot in range(SIDE)]
    high = lambda spot: held_up[there[spot]] + came_up[there[spot]]
    low = lambda spot: held_down[there[spot]] + came_down[there[spot]]
    up[...] = low(1)
    down[...] = high(3)
    kept_up[...] = high(1)
    kept_down[...] = low(3)
    own[:depth, :] = high(0)
    own[depth:, :] = low(0)


def turn(coords, pairs, after):
    depth, width = pairs[0][0].shape[1:]
    part, terms = shape(depth, width), [*pairs[0], *pairs[1]]
    first = run(turn_first_kernel, [part] * 2, coords, terms, after, "turn_first")
    outs = [part] * 4 + [shape(2 * depth, width)]
    return [*first, *run(turn_rest_kernel, outs, coords, terms, first[0], "turn_rest")]


def ring_add_kernel(mine_up, came_up, mine_down, came_down, up_ref, down_ref):
    up_ref[...] = mine_up[...] + came_up[...]
    down_ref[...] = mine_down[...] + came_down[...]


def pieces_of(values):
    high = values.astype(jnp.bfloat16)
    rest = values - high.astype(jnp.float32)
    middle = rest.astype(jnp.bfloat16)
    low = (rest - middle.astype(jnp.float32)).astype(jnp.bfloat16)
    return high, middle, low


def stacked(values, order):
    pieces = pieces_of(values)
    return [pieces[index] for index in order]


LEFT_ORDER, RIGHT_ORDER = (0, 0, 1, 1, 0, 2), (0, 1, 0, 1, 2, 0)


def left_kernel(
    scalar_ref, partial_ref, basis_ref, error_ref, after_ref, keep_ref, send_ref, copy_ref, pieces, total
):
    step = pl.program_id(0)
    count, own = basis_ref.shape[0], error_ref.shape[0]
    size = partial_ref.shape[0]
    half = count // 2
    across = (((1,), (1,)), ((), ()))

    @pl.when(step == 0)
    def _():
        for index, piece in enumerate(pieces_of(basis_ref[...])):
            pieces[index * count : (index + 1) * count, :] = piece

    copy_ref[...] = partial_ref[...]
    three = lax.dot_general(pieces[...], partial_ref[...], across, preferred_element_type=jnp.float32)
    total[:, span(step, size)] = three[:count] + (three[count : 2 * count] + three[2 * count :])

    @pl.when(step == pl.num_programs(0) - 1)
    def _():
        shard, core = scalar_ref[0], scalar_ref[1]
        terms = jnp.concatenate(pieces_of(error_ref[...]), axis=0)
        nine = lax.dot_general(pieces[...], terms, across, preferred_element_type=jnp.float32)
        block = lambda i, j: nine[i * count : (i + 1) * count, j * own : (j + 1) * own]
        kept = block(0, 0) + ((block(0, 1) + block(1, 0)) + (block(1, 1) + (block(0, 2) + block(2, 0))))
        wide = jnp.concatenate([kept] * (LANES // own), axis=1)
        lane = lax.broadcasted_iota(jnp.int32, wide.shape, 1)
        there = span(shard // (LANES // own), LANES)
        total[:, there] += jnp.where(lane // own == shard % (LANES // own), wide, 0.0)
        keep_ref[...] = total[span(core, half), :]
        send_ref[...] = total[span(1 - core, half), :]


def left_terms(scalars, partial, basis, error, after):
    rows, width = partial.shape
    count = basis.shape[0]
    size = rows // SIDE
    fixed = lambda k: (0, 0)
    return pl.pallas_call(
        left_kernel,
        grid=(SIDE,),
        in_specs=[
            SCALARS,
            pl.BlockSpec((size, width), lambda k: (k, 0)),
            pl.BlockSpec(basis.shape, fixed, pipeline_mode=ONCE),
            pl.BlockSpec(error.shape, fixed, pipeline_mode=ONCE),
            ANY,
        ],
        out_specs=[pl.BlockSpec((count // 2, rows), fixed)] * 2
        + [pl.BlockSpec((size, width), lambda k: (k, 0))],
        out_shape=[shape(count // 2, rows)] * 2 + [shape(rows, width, dtype=partial.dtype)],
        scratch_shapes=[pltpu.VMEM((3 * count, width), jnp.bfloat16), pltpu.VMEM((count, rows), jnp.float32)],
        cost_estimate=FREE,
        compiler_params=limit(16),
        name="left_terms",
    )(scalars, partial, basis, error, after)


def ordered(core, mine, other):
    return jnp.where(core == 0, mine, other), jnp.where(core == 0, other, mine)


def orthonormal_kernel(scalar_ref, mine_ref, other_ref, out_ref, pieces_ref):
    mat = jnp.concatenate(ordered(1 - scalar_ref[1], mine_ref[...], other_ref[...]), axis=0)
    count = mat.shape[0]
    size = SUBLANES
    groups = [mat[start : start + size, :] for start in range(0, count, size)]
    order = lax.broadcasted_iota(jnp.int32, (size, 1), 0)
    for index in range(count):
        group, spot = index // size, index % size
        column = groups[group][spot : spot + 1, :]
        products = [jnp.sum(later * column, axis=1, keepdims=True) for later in groups[group:]]
        own_norm = products[0][spot : spot + 1, :]
        weights = [product / own_norm for product in products]
        weights[0] = jnp.where(order > spot, weights[0], 0.0)
        scaled = column / jnp.sqrt(own_norm)
        groups[group:] = [later - weight * column for later, weight in zip(groups[group:], weights)]
        groups[group] = jnp.where(order == spot, scaled, groups[group])
    mat = jnp.concatenate(groups, axis=0)
    out_ref[...] = mat
    for index, piece in enumerate(pieces_of(mat)):
        pieces_ref[index * count : (index + 1) * count, :] = piece


def own_rows(phat, shard, own):
    parts = [phat[:, start : start + own] for start in range(0, LANES, own)]
    chosen = parts[0]
    for index, part in enumerate(parts[1:], 1):
        chosen = jnp.where(shard % (LANES // own) == index, part, chosen)
    return chosen


def right_kernel(scalar_ref, pieces_ref, partial_ref, phat_ref, error_ref, after_ref, keep_ref, send_ref, total):
    step = pl.program_id(0)
    count, own = phat_ref.shape[0], error_ref.shape[0]
    width = partial_ref.shape[1]
    half = count // 2
    three = jnp.dot(pieces_ref[...], partial_ref[...], preferred_element_type=jnp.float32)
    terms = three[:count] + (three[count : 2 * count] + three[2 * count :])

    @pl.when(step == 0)
    def _():
        shard = scalar_ref[0]
        mine = own_rows(phat_ref[:, span(shard // (LANES // own), LANES)], shard, own)
        total[:, :width] = terms + jnp.dot(
            mine, error_ref[...], precision=HIGHEST, preferred_element_type=jnp.float32
        )
        total[:, width:] = jnp.zeros((count, total.shape[1] - width), jnp.float32)

    @pl.when(step > 0)
    def _():
        total[:, :width] += terms

    @pl.when(step == pl.num_programs(0) - 1)
    def _():
        core = scalar_ref[1]
        keep_ref[...] = total[span(core, half), :]
        send_ref[...] = total[span(1 - core, half), :]


def right_terms(scalars, pieces, partial, phat, error, after):
    rows, width = partial.shape
    count = phat.shape[0]
    padded = -(-width // (LANES * SIDE)) * LANES * SIDE
    size = rows // SIDE
    fixed = lambda k: (0, 0)
    return pl.pallas_call(
        right_kernel,
        grid=(SIDE,),
        in_specs=[
            SCALARS,
            pl.BlockSpec((3 * count, size), lambda k: (0, k)),
            pl.BlockSpec((size, width), lambda k: (k, 0)),
            pl.BlockSpec(phat.shape, fixed, pipeline_mode=ONCE),
            pl.BlockSpec(error.shape, fixed, pipeline_mode=ONCE),
            ANY,
        ],
        out_specs=[pl.BlockSpec((count // 2, padded), fixed)] * 2,
        out_shape=[shape(count // 2, padded)] * 2,
        scratch_shapes=[pltpu.VMEM((count, padded), jnp.float32)],
        cost_estimate=FREE,
        compiler_params=limit(12),
        name="right_terms",
    )(scalars, pieces, partial, phat, error, after)


def gate(arrays, after):
    return pl.pallas_call(
        lambda *refs: None,
        in_specs=[ANY] * (len(arrays) + len(after)),
        out_specs=[ANY] * len(arrays),
        out_shape=[shape(*array.shape) for array in arrays],
        input_output_aliases={index: index for index in range(len(arrays))},
        cost_estimate=FREE,
        compiler_params=limit(1),
        name="gate",
    )(*arrays, *after)


def add_kernel(*refs):
    terms = [ref[...] for ref in refs[:-1]]
    refs[-1][...] = sum(terms[1:], terms[0])


def add(terms, after):
    return run(add_kernel, [shape(*terms[0].shape)], None, terms, after, "add", room=1)[0]


def add_four_kernel(a_ref, b_ref, c_ref, d_ref, out_ref):
    out_ref[...] = (a_ref[...] + b_ref[...]) + (c_ref[...] + d_ref[...])


def sum_four(values, along, after):
    return sum_came(values, [along(values, step) for step in (2, 1, -1)], after)


def sum_came(values, came, after):
    outs = [shape(*values.shape)]
    return run(add_four_kernel, outs, None, [values, *came], after, "add_four", room=1)[0]


def sum_pairs(values, pairs, after):
    for mask in (1, 3):
        values = after = add([values, pairs(values, mask)], after)
    return values


def add_cut_kernel(scalar_ref, a_ref, b_ref, *out_refs):
    x, size = scalar_ref[2], out_refs[0].shape[1]
    for index, out_ref in enumerate(out_refs):
        there = span(lax.rem(x + index, SIDE), size)
        out_ref[...] = a_ref[:, there] + b_ref[:, there]


def scatter_x(scalars, keep, came, after):
    outs = [shape(keep.shape[0], keep.shape[1] // SIDE)] * SIDE
    parts = run(add_cut_kernel, outs, scalars, [keep, came], after, "add_cut")
    came = [along_x(parts[2], 2), along_x(parts[1], 1), along_x(parts[3], -1)]
    return run(add_four_kernel, outs[:1], None, [parts[0], *came], parts[0], "add_four", room=1)[0]


def join_two_kernel(a_ref, b_ref, out_ref):
    size = a_ref.shape[1]
    out_ref[:, :size] = a_ref[...]
    out_ref[:, size:] = b_ref[...]


def join_four_kernel(scalar_ref, mine_ref, came_ref, out_ref):
    x, size = scalar_ref[2], mine_ref.shape[1] // 2
    for ref, masks in ((mine_ref, (0, 3)), (came_ref, (1, 2))):
        for index, mask in enumerate(masks):
            out_ref[:, span(x ^ mask, size)] = ref[:, index * size : (index + 1) * size]


def product(left, right, replicas):
    total = lax.dot_general(
        jnp.concatenate(stacked(left, LEFT_ORDER), axis=0),
        jnp.concatenate(stacked(right, RIGHT_ORDER), axis=0),
        (((0,), (0,)), ((), ())),
        preferred_element_type=jnp.float32,
    )
    return total * (1.0 / replicas)


def half_product(replicas, scalar_ref, half, values_ref, phat_ref, own, width):
    shard, count = scalar_ref[0], values_ref.shape[0]
    mine = own_rows(phat_ref[span(half, count), span(shard // (LANES // own), LANES)], shard, own)
    return product(mine, values_ref[:, :width], replicas)


def nearly_kernel(replicas, scalar_ref, mine_ref, phat_ref, error_ref, kept_ref, up_ref, down_ref, *out_refs):
    half_ref, rest_ref = out_refs
    own, width = error_ref.shape
    approx = half_product(replicas, scalar_ref, scalar_ref[1], mine_ref, phat_ref, own, width)
    half_ref[...] = approx
    depth = own // 2
    for rows, came_ref in ((slice(0, depth), down_ref), (slice(depth, own), up_ref)):
        rest_ref[rows, :] = (error_ref[rows, :] + (kept_ref[rows, :] + came_ref[...])) - approx[rows, :]


def finish_kernel(replicas, scalar_ref, mine_ref, other_ref, phat_ref, half_ref, rest_ref, *refs):
    up_ref, down_ref, grad_out, next_out, basis_out, grad_ref, next_ref, basis_ref, sent = refs
    core = scalar_ref[1]
    own, width = rest_ref.shape
    count, depth = mine_ref.shape[0], own // 2
    basis_ref[span(core, count), :] = mine_ref[:, :width] * (1.0 / replicas)
    basis_ref[span(1 - core, count), :] = other_ref[:, :width] * (1.0 / replicas)
    copies = [pltpu.make_async_copy(basis_ref, basis_out, sent.at[0])]
    copies[-1].start()
    approx = half_product(replicas, scalar_ref, 1 - core, other_ref, phat_ref, own, width)
    for index, came_ref in enumerate((up_ref, down_ref)):
        rows = slice(index * depth, (index + 1) * depth)
        there = pl.ds(index * depth, depth)
        next_ref[rows, :] = (rest_ref[rows, :] + came_ref[...]) - approx[rows, :]
        copies.append(pltpu.make_async_copy(next_ref.at[there, :], next_out.at[there, :], sent.at[1 + index]))
        copies[-1].start()
    grad_ref[...] = (half_ref[...] + approx).astype(jnp.bfloat16)
    copies.append(pltpu.make_async_copy(grad_ref, grad_out, sent.at[3]))
    copies[-1].start()
    for copy in copies:
        copy.wait()


def finish(replicas, outs, scalars, operands):
    return pl.pallas_call(
        functools.partial(finish_kernel, replicas),
        in_specs=[SCALARS] + [WHOLE] * len(operands),
        out_specs=[ANY] * len(outs),
        out_shape=outs,
        scratch_shapes=[pltpu.VMEM(out.shape, out.dtype) for out in outs]
        + [pltpu.SemaphoreType.DMA((4,))],
        cost_estimate=FREE,
        compiler_params=limit(10),
        name="finish",
    )(scalars, *operands)


def shards(partials, error, basis):
    replicas = lax.axis_size("dp")
    dp, shard = lax.axis_index("dp"), lax.axis_index("shard")
    x, core = dp // 2, dp % 2
    partial, error, basis = partials[0, 0], error[0], basis.T
    rows, width = partial.shape
    own, count = error.shape[0], basis.shape[0]
    depth = own // 2
    scalars = jnp.stack([shard, core, x]).astype(jnp.int32)
    z, y = shard // SIDE, shard % SIDE
    first, second = jnp.where(core == 0, z, y), jnp.where(core == 0, y, z)
    near = jnp.arange(SIDE)
    coords = jnp.concatenate([(first + near) % SIDE, (second + near) % SIDE, core[None]])
    coords = coords.astype(jnp.int32)
    large = in_hbm(partial.reshape(SIDE, SIDE, 2, own // 2, width))

    sent1 = first_blocks(large, coords, scalars)
    came1 = [along_first(sent1[0], 1), along_first(sent1[1], -1)]
    keep, send, partial = left_terms(scalars, in_hbm(partial), basis, error, sent1[0])
    blocks = partial.reshape(SIDE, SIDE, 4, own // 4, width)
    part = add([keep, other_core(send)], keep)
    sent2 = combine(blocks, coords, [(1, 1, []), (3, 0, [])], part)
    part = sum_four(part, along_x, sent2[0])
    sent2 = gate(sent2, [part])
    came2 = [along_first(sent2[0], 1), along_first(sent2[1], -1)]
    part = sum_pairs(part, pair_second, sent2[0])
    sent3 = combine(blocks, coords, [(1, 0, [came1[0]]), (3, 1, [came1[1]])], part)
    (part,) = gate([other_core(part)], [sent3[0]])
    part = sum_four(part, along_second, part)
    sent3 = gate(sent3, [part])
    came3 = [along_first(sent3[0], 1), along_first(sent3[1], -1)]
    phat, pieces = run(
        orthonormal_kernel,
        [shape(count, rows), shape(3 * count, rows, dtype=jnp.bfloat16)],
        scalars,
        [part, other_core(part)],
        sent3[0],
        "orthonormal",
    )
    keep, send = right_terms(scalars, pieces, partial, phat, error, phat)
    held = combine(blocks, coords, [(0, 0, [came2[1]]), (0, 1, [came2[0]])], send)
    part = scatter_x(scalars, keep, other_core(send), held[0])
    part = sum_four(part, along_second, part)
    came = [along_first(part, step) for step in (2, 1, -1)]
    up, down, up_local, down_local, kept_up, kept_down, kept = turn(
        coords, [(held[0], came3[0]), (held[1], came3[1])], came[:2]
    )
    came4 = [along_second(up, 1), along_second(down, -1)]
    came5 = [along_second(up_local, 1), along_second(down_local, -1)]
    part = sum_came(part, came, up)
    pair = run(join_two_kernel, [shape(count // 2, 2 * part.shape[1])], None, [part, pair_x(part, 3)], part, "join", room=1)[0]
    sent6 = run(
        ring_add_kernel,
        [shape(own // 2, width)] * 2,
        None,
        [kept_up, came4[0], kept_down, came4[1]],
        pair,
        "ring_add",
    )
    came6 = [along_second(sent6[0], 1), along_second(sent6[1], -1)]
    outs = [shape(count // 2, 2 * pair.shape[1])]
    part = run(join_four_kernel, outs, scalars, [pair, pair_x(pair, 1)], sent6[0], "join")[0]
    half, rest = run(
        functools.partial(nearly_kernel, replicas),
        [shape(own, width)] * 2,
        scalars,
        [part, phat, error, kept, *came5],
        part,
        "nearly",
    )
    grad, following, right = finish(
        replicas,
        [shape(own, width, dtype=jnp.bfloat16), shape(own, width), shape(count, width)],
        scalars,
        [part, other_core(part), phat, half, rest, *came6],
    )
    return grad, following[None], right.T


def solution(mesh):
    return jax.shard_map(
        shards,
        mesh=mesh,
        in_specs=(P("dp", "shard", None, None), P("dp", "shard", None), P()),
        out_specs=(P("shard", None), P("dp", "shard", None), P()),
        check_vma=False,
    )
```
